32 devices in a mesh: ka: 8 (over z, y), ga: 4 (over x, core).
Axes of the slice: x: 2, y: 2, z: 4, core: 2. Of those that a mesh axis runs over, the one named last changes fastest.
Arguments:
- cond: bfloat16 [8, 8, 4096], P('ka', None, 'ga'), may hold values from -6 to 6
- vale: bfloat16 [8, 8, 4096], P('ka', None, 'ga'), may hold values from -6 to 6
- screen: bfloat16 [8, 4096, 4096], P('ka', 'ga'), may hold values from -0.0014648438 to 0.0014648438
- qtable: int32 [8, 8], replicated, may hold values from 0 to 7, as said below
- gmap: int32 [8, 4096], P('ka', 'ga'), may hold values from 0 to 4095, as said below
Outputs:
- kernel: float32 [8, 3, 4096], P('ka', None, 'ga')
The draws below stay inside these ranges and needn't reach their ends.
Inputs may be any that keep to these rules, and one draw needn't show every extreme that they name: qtable[k,k2] depends only on (k - k2) mod 8, and each row names every k-difference once. `gmap`: each aligned block of 1024 entries of a row is an ordering of that block's own grid indices.
All inputs are finite; a program needn't handle non-finite values.
Results may differ from the reference program's by a relative error of at most 0.0041.
Values may be sent and summed in bfloat16 or wider, within the bound.
A program may use at most 128 MiB of HBM per device.

```python
import jax
import jax.numpy as jnp
from jax import lax

NG = 4096
NC = 8
NV = 8
NSHIFT = 2
KPTS = 8
GDEV = 1024
N_KA = 8


def draw_qtable(key, part):
    key = jax.random.fold_in(key, 1)
    order = jax.random.permutation(key, KPTS).astype(jnp.int32)
    rows = jnp.arange(KPTS, dtype=jnp.int32)
    diff = (rows[:, None] - rows[None, :]) % KPTS
    return order[diff].astype(jnp.int32)


def draw_gmap(key, part):
    key = jax.random.fold_in(key, 2)
    blocks = NG // GDEV
    scores = jax.random.randint(key, (KPTS, blocks, GDEV), 0, 2 ** 16, dtype=jnp.int32)
    scores = scores * GDEV + jnp.arange(GDEV, dtype=jnp.int32)[None, None, :]
    order = jnp.argsort(scores, axis=2, stable=True).astype(jnp.int32)
    base = (jnp.arange(blocks, dtype=jnp.int32) * GDEV)[None, :, None]
    return (order + base).reshape(KPTS, NG).astype(jnp.int32)


def shard_levels(rng, shape, cuts, least, top_value):
    level, own = 1.0, jax.random.fold_in(rng, 6)
    for position, blocks in cuts:
        draws = jnp.exp(jax.random.uniform(jax.random.fold_in(own, position), (blocks,), jnp.float32, least / len(cuts), top_value / len(cuts)))
        level = level * jnp.repeat(draws, shape[position] // blocks).reshape([-1 if axis == position else 1 for axis in range(len(shape))])
    return level


def gaussian(rng, dims, width, limit, shards=(), held_as=jnp.bfloat16):
    array = width * jax.random.normal(rng, dims, jnp.float32)
    if shards:
        array = array * shard_levels(rng, dims, shards, -0.22, 0.18)
    return jnp.clip(array, -limit, limit).astype(held_as)


def setup_inputs(seed: int = 0) -> dict:
    arg_keys = jax.random.split(jax.random.key(seed), 6)
    return {
        "cond": gaussian(arg_keys[0], (KPTS, NC, NG), 1.0, 6.0, ((0, 8), (2, 4))),
        "vale": gaussian(arg_keys[1], (KPTS, NV, NG), 1.0, 6.0, ((0, 8), (2, 4))),
        "screen": gaussian(arg_keys[2], (KPTS, NG, NG), (NG * NG) ** -0.5, 0.0014648438, ((0, 8), (1, 4))),
        "qtable": draw_qtable(jax.random.fold_in(arg_keys[5], 71), 0),
        "gmap": draw_gmap(jax.random.fold_in(arg_keys[5], 71), 0),
    }


def pair_density(own, far):
    product = own.astype(jnp.float32)[:, None, :] * far.astype(jnp.float32)[None, :, :]
    return product.astype(jnp.bfloat16).reshape(-1, own.shape[-1])


def reference(cond, vale, screen, qtable, gmap):
    k_rows = KPTS // N_KA
    indices = jnp.arange(KPTS, dtype=jnp.int32)
    cond_mapped = jnp.take_along_axis(cond, gmap[:, None, :], axis=2)
    vale_mapped = jnp.take_along_axis(vale, gmap[:, None, :], axis=2)
    blocks = []
    for offset in range(NSHIFT + 1):
        for right in range(k_rows):
            partner = (((indices // k_rows - offset) % N_KA) * k_rows + right).astype(jnp.int32)

            def one_row(row, partner=partner):
                other = partner[row]
                qindex = qtable[row, other]
                weight = lax.dynamic_index_in_dim(screen, qindex, 0, keepdims=False)
                dens_c = pair_density(cond[row], cond_mapped[other])
                dens_v = pair_density(vale[row], vale_mapped[other])
                image = jnp.dot(weight, dens_v.T, preferred_element_type=jnp.float32)
                tile = jnp.dot(dens_c.astype(jnp.float32), image, precision=lax.Precision.HIGHEST)
                return tile.reshape(-1)

            blocks.append(lax.map(one_row, indices))
    return jnp.stack(blocks, axis=1)
```

```python
import functools

import jax
import jax.numpy as jnp
from jax import lax
from jax.experimental import pallas as pl
from jax.experimental.pallas import tpu as pltpu
from jax.sharding import PartitionSpec as P

NSHIFT = 2
MESH = pl.DeviceIdType.MESH
F32 = jnp.float32
BF16 = jnp.bfloat16


def flipped(index, bit):
    width = 1 << bit
    return index + width * (1 - 2 * ((index // width) % 2))


def moved(index, offset, bits):
    for bit in range(bits):
        if (offset >> bit) & 1:
            index = flipped(index, bit)
    return index


def ring_place(ka, peers):
    y, z = ka % 2, ka // 2
    return z * (1 - y) + (peers - 1 - z) * y


def ring_member(place, peers):
    place = (place + 2 * peers) % peers
    late = place // (peers // 2)
    return (1 - late) * 2 * place + late * (2 * (peers - 1 - place) + 1)


def densities(own, far):
    product = own.astype(F32)[:, None, :] * far.astype(F32)[None, :, :]
    return product.reshape(-1, own.shape[-1]).astype(BF16)


def kernel(
    n_k, n_g, cond, vale, screen, qtable, gmap, out,
    s_held, c_all, pc, tiles, sent, got,
    s_sem, c_send, c_recv, v_send, v_recv, g_send, g_recv, t_send, t_recv, *v_from,
):
    bits = n_g.bit_length() - 1
    total = n_k * n_g
    width = cond.shape[2]
    n_c = cond.shape[1]
    rows = n_c * n_c
    me_k, me_g = lax.axis_index("ka"), lax.axis_index("ga")
    me = me_k * n_g + me_g

    barrier = pltpu.get_barrier_semaphore()

    def greet(step, carry):
        peer = (me + step) % total
        pl.semaphore_signal(
            barrier, inc=1, device_id=(peer // n_g, peer % n_g), device_id_type=MESH
        )
        return carry

    lax.fori_loop(1, total, greet, 0)

    loads = []
    for offset in range(n_g):
        block = moved(me_g, offset, bits)
        load = pltpu.make_async_copy(
            screen.at[0, :, pl.ds(pl.multiple_of(block * width, width), width)],
            s_held.at[block],
            s_sem.at[offset],
        )
        load.start()
        loads.append(load)

    local_map = gmap[...] - me_g * width
    both = jnp.concatenate([cond[0], vale[0]], axis=0)
    part = min(256, width)
    mapped = jnp.zeros((2 * n_c, width), F32)
    for first in range(0, width, part):
        points = lax.broadcasted_iota(jnp.int32, (part, width), 0) + first
        pick = jnp.where(points == local_map, 1.0, 0.0).astype(BF16)
        mapped += jnp.dot(both[:, first : first + part], pick, preferred_element_type=F32)
    mapped = mapped.astype(BF16)
    c_all[me_k] = jnp.concatenate([cond[0], mapped[:n_c]], axis=0)
    v_from[0][me_k] = jnp.concatenate([vale[0], mapped[n_c:]], axis=0)

    pl.semaphore_wait(barrier, total - 1)

    place = ring_place(me_k, n_k)
    right, left = ring_member(place + 1, n_k), ring_member(place - 1, n_k)
    n_right, n_left = n_k // 2, n_k - 1 - n_k // 2

    def c_copy(chunk, slot, target):
        return pltpu.make_async_remote_copy(
            src_ref=c_all.at[chunk], dst_ref=c_all.at[chunk],
            send_sem=c_send.at[slot], recv_sem=c_recv.at[chunk],
            device_id=(target, me_g), device_id_type=MESH,
        )

    def v_copy(chunk, slot, target):
        return pltpu.make_async_remote_copy(
            src_ref=v_from[0].at[chunk], dst_ref=v_from[0].at[chunk],
            send_sem=v_send.at[slot], recv_sem=v_recv.at[chunk],
            device_id=(target, me_g), device_id_type=MESH,
        )

    def across(chunk):
        for bit in reversed(range(bits)):
            pltpu.make_async_remote_copy(
                src_ref=v_from[0].at[chunk], dst_ref=v_from[1 << bit].at[chunk],
                send_sem=g_send.at[1 << bit], recv_sem=g_recv.at[1 << bit],
                device_id=(me_k, flipped(me_g, bit)), device_id_type=MESH,
            ).start()

    def whole_block(offset, bit):
        return pltpu.make_async_remote_copy(
            src_ref=v_from[offset], dst_ref=v_from[offset | (1 << bit)],
            send_sem=g_send.at[offset | (1 << bit)], recv_sem=g_recv.at[offset | (1 << bit)],
            device_id=(me_k, flipped(me_g, bit)), device_id_type=MESH,
        )

    c_copy(me_k, 0, right).start()
    c_copy(me_k, n_right, left).start()
    v_copy(me_k, 0, right).start()
    v_copy(me_k, n_right, left).start()
    across(me_k)
    for step in range(1, n_right + 1):
        from_left = ring_member(place - step, n_k)
        from_right = ring_member(place + step, n_k)
        c_copy(from_left, 0, right).wait_recv()
        if step < n_right:
            c_copy(from_left, step, right).start()
        if step <= n_left:
            c_copy(from_right, 0, left).wait_recv()
            if step < n_left:
                c_copy(from_right, n_right + step, left).start()
        v_copy(from_left, 0, right).wait_recv()
        if step < n_right:
            v_copy(from_left, step, right).start()
        across(from_left)
        if step <= n_left:
            v_copy(from_right, 0, left).wait_recv()
            if step < n_left:
                v_copy(from_right, n_right + step, left).start()
            across(from_right)

    shift = jnp.int32(0)
    for row in range(n_k):
        shift = jnp.where(qtable[row, 0] == me_k, row, shift)

    def build(k, carry):
        partner = lax.rem(k - shift + n_k, n_k)
        dens = densities(c_all[k][:n_c], c_all[partner][n_c:])
        pc[pl.ds(pl.multiple_of(k * rows, rows), rows), :] = dens
        return carry

    lax.fori_loop(0, n_k, build, 0)
    tiles[...] = jnp.zeros_like(tiles)

    sub = min(512, width)
    unit = 8
    group = 4
    for offset in range(n_g):
        block = moved(me_g, offset, bits)
        loads[offset].wait()
        if offset:
            low = (offset & -offset).bit_length() - 1
            whole_block(offset & (offset - 1), low).wait_recv()
            for bit in reversed(range(low)):
                whole_block(offset, bit).start()

        def step(number, carry, block=block, held=v_from[offset]):
            which, column = number // (width // sub), number % (width // sub)
            columns = pl.ds(pl.multiple_of(column * sub, sub), sub)
            left_rows = pl.ds(pl.multiple_of(which * (unit * rows), unit * rows), unit * rows)
            weighted = jnp.dot(
                pc[left_rows, :], s_held[block, :, columns], preferred_element_type=F32
            ).astype(BF16)
            for part in range(unit // group):
                dens = []
                for k in range(group):
                    k = which * unit + part * group + k
                    partner = lax.rem(k - shift + n_k, n_k)
                    own = held[k, :, columns][:n_c]
                    far = held[partner, :, columns][n_c:]
                    dens.append(densities(own, far))
                tiles[which * (unit // group) + part] += lax.dot_general(
                    weighted[part * group * rows : (part + 1) * group * rows],
                    jnp.concatenate(dens, axis=0),
                    (((1,), (1,)), ((), ())),
                    preferred_element_type=F32,
                )
            return carry

        lax.fori_loop(0, (n_k // unit) * (width // sub), step, 0)

    share = rows // n_g
    half = share // 2

    def lay_out(which, carry):
        for k in range(group):
            for to in range(n_g):
                first = k * rows + to * share
                lanes = slice(k * rows, (k + 1) * rows)
                sent[(which * group + k) * n_g + to] = jnp.concatenate(
                    [
                        tiles[which, first : first + half, lanes],
                        tiles[which, first + half : first + share, lanes],
                    ],
                    axis=1,
                )
        return carry

    lax.fori_loop(0, n_k // group, lay_out, 0)

    def hand_out(step, carry):
        peer = (me + step) % total
        pltpu.make_async_remote_copy(
            src_ref=sent.at[peer], dst_ref=got.at[me],
            send_sem=t_send, recv_sem=t_recv,
            device_id=(peer // n_g, peer % n_g), device_id_type=MESH,
        ).start()
        return carry

    lax.fori_loop(1, total, hand_out, 0)
    got[me] = sent[me]

    for slot in range(n_k - 1):
        c_copy(me_k, slot, right).wait_send()
        v_copy(me_k, slot, right).wait_send()
    for offset in range(1, n_g):
        low = (offset & -offset).bit_length() - 1
        whole_block(offset & (offset - 1), low).wait_send()

    handed = pltpu.make_async_remote_copy(
        src_ref=sent.at[pl.ds(0, total - 1)], dst_ref=got.at[pl.ds(0, total - 1)],
        send_sem=t_send, recv_sem=t_recv,
        device_id=(me_k, flipped(me_g, 0)), device_id_type=MESH,
    )
    handed.wait_recv()
    for number in range(NSHIFT + 1):
        holder = qtable[number, 0]
        value = got[holder * n_g]
        for source in range(1, n_g):
            value += got[holder * n_g + source]
        out[number, :half, :] = value[:, :rows]
        out[number, half:, :] = value[:, rows:]
    handed.wait_send()


def per_device(cond, vale, screen, qtable, gmap):
    n_k, n_g = lax.axis_size("ka"), lax.axis_size("ga")
    n_c, width = cond.shape[1], cond.shape[2]
    rows = n_c * n_c
    share = rows // n_g
    total = n_k * n_g
    vmem = pl.BlockSpec(memory_space=pltpu.VMEM)
    dma = pltpu.SemaphoreType.DMA
    result = pl.pallas_call(
        functools.partial(kernel, n_k, n_g),
        out_shape=jax.ShapeDtypeStruct((NSHIFT + 1, share, rows), F32),
        in_specs=[
            vmem, vmem, pl.BlockSpec(memory_space=pl.ANY),
            pl.BlockSpec(memory_space=pltpu.SMEM), vmem,
        ],
        out_specs=vmem,
        scratch_shapes=[
            pltpu.VMEM((n_g, width, width), BF16),
            pltpu.VMEM((n_k, 2 * n_c, width), BF16),
            pltpu.VMEM((n_k * rows, width), BF16),
            pltpu.VMEM((n_k // 4, 4 * rows, 4 * rows), F32),
            pltpu.VMEM((total, share // 2, 2 * rows), F32),
            pltpu.VMEM((total, share // 2, 2 * rows), F32),
            dma((n_g,)), dma((n_k,)), dma((n_k,)), dma((n_k,)), dma((n_k,)),
            dma((n_g,)), dma((n_g,)), dma(()), dma(()),
        ]
        + [pltpu.VMEM((n_k, 2 * n_c, width), BF16)] * n_g,
        compiler_params=pltpu.CompilerParams(
            collective_id=0, has_side_effects=True, vmem_limit_bytes=48 * 1024 * 1024
        ),
        cost_estimate=pl.CostEstimate(
            flops=2 * n_k * rows * width * screen.shape[2],
            bytes_accessed=2 * width * screen.shape[2],
            transcendentals=0,
        ),
    )(cond, vale, screen, qtable, gmap)
    return result.reshape(1, NSHIFT + 1, share * rows)


def solution(mesh):
    in_specs = (P("ka", None, "ga"), P("ka", None, "ga"), P("ka", "ga", None), P(), P("ka", "ga"))
    out_specs = P("ka", None, "ga")
    return jax.shard_map(
        per_device, mesh=mesh, in_specs=in_specs, out_specs=out_specs, check_vma=False
    )
```

```python
import functools

import jax
import jax.numpy as jnp
from jax import lax
from jax.experimental import pallas as pl
from jax.experimental.pallas import tpu as pltpu
from jax.sharding import PartitionSpec as P

NSHIFT = 2
MESH = pl.DeviceIdType.MESH
F32 = jnp.float32
BF16 = jnp.bfloat16


def flipped(index, bit):
    width = 1 << bit
    return index + width * (1 - 2 * ((index // width) % 2))


def moved(index, offset, bits):
    for bit in range(bits):
        if (offset >> bit) & 1:
            index = flipped(index, bit)
    return index


def ring_place(ka, peers):
    y, z = ka % 2, ka // 2
    return z * (1 - y) + (peers - 1 - z) * y


def ring_member(place, peers):
    place = (place + 2 * peers) % peers
    late = place // (peers // 2)
    return (1 - late) * 2 * place + late * (2 * (peers - 1 - place) + 1)


def densities(own, far):
    product = own.astype(F32)[:, None, :] * far.astype(F32)[None, :, :]
    return product.reshape(-1, own.shape[-1]).astype(BF16)


def kernel(
    n_k, n_g, cond_in, vale_in, screen, qtable_in, gmap_in, out,
    cond, vale, qtable, gmap, s_held, c_all, pc, tiles, sent, got, summed, came,
    in_sem, s_sem, c_send, c_recv, v_send, v_recv, g_send, g_recv,
    p_send, p_recv, t_send, t_recv, *blocks,
):
    v_from, w_from = blocks[:n_g], blocks[n_g:]
    bits = n_g.bit_length() - 1
    width = cond.shape[2]
    n_c = cond.shape[1]
    rows = n_c * n_c
    me_k, me_g = lax.axis_index("ka"), lax.axis_index("ga")

    arrivals = [
        pltpu.make_async_copy(source, target, in_sem.at[number])
        for number, (source, target) in enumerate(
            [(gmap_in, gmap), (cond_in, cond), (vale_in, vale), (qtable_in, qtable)]
        )
    ]
    for arrival in arrivals:
        arrival.start()

    barrier = pltpu.get_barrier_semaphore()

    def greet_k(step, carry):
        pl.semaphore_signal(
            barrier, inc=1, device_id=((me_k + step) % n_k, me_g), device_id_type=MESH
        )
        return carry

    def greet_g(step, carry):
        pl.semaphore_signal(
            barrier, inc=1, device_id=(me_k, (me_g + step) % n_g), device_id_type=MESH
        )
        return carry

    lax.fori_loop(1, n_k, greet_k, 0)
    lax.fori_loop(1, n_g, greet_g, 0)

    for arrival in arrivals:
        arrival.wait()

    loads = []
    for offset in range(n_g):
        block = moved(me_g, offset, bits)
        load = pltpu.make_async_copy(
            screen.at[0, :, pl.ds(pl.multiple_of(block * width, width), width)],
            s_held.at[block],
            s_sem.at[offset],
        )
        load.start()
        loads.append(load)

    local_map = gmap[...] - me_g * width
    both = jnp.concatenate([cond[0], vale[0]], axis=0)
    part = min(256, width)
    mapped = jnp.zeros((2 * n_c, width), F32)
    for first in range(0, width, part):
        points = lax.broadcasted_iota(jnp.int32, (part, width), 0) + first
        pick = jnp.where(points == local_map, 1.0, 0.0).astype(BF16)
        mapped += jnp.dot(both[:, first : first + part], pick, preferred_element_type=F32)
    mapped = mapped.astype(BF16)
    c_all[me_k] = jnp.concatenate([cond[0], mapped[:n_c]], axis=0)
    v_from[0][me_k] = jnp.concatenate([vale[0], mapped[n_c:]], axis=0)

    pl.semaphore_wait(barrier, n_k + n_g - 2)

    place = ring_place(me_k, n_k)
    right, left = ring_member(place + 1, n_k), ring_member(place - 1, n_k)
    n_right, n_left = n_k // 2, n_k - 1 - n_k // 2

    def c_copy(chunk, slot, target):
        return pltpu.make_async_remote_copy(
            src_ref=c_all.at[chunk], dst_ref=c_all.at[chunk],
            send_sem=c_send.at[slot], recv_sem=c_recv.at[chunk],
            device_id=(target, me_g), device_id_type=MESH,
        )

    def v_copy(chunk, slot, target):
        return pltpu.make_async_remote_copy(
            src_ref=v_from[0].at[chunk], dst_ref=v_from[0].at[chunk],
            send_sem=v_send.at[slot], recv_sem=v_recv.at[chunk],
            device_id=(target, me_g), device_id_type=MESH,
        )

    def across(chunk):
        for bit in reversed(range(bits)):
            pltpu.make_async_remote_copy(
                src_ref=v_from[0].at[chunk], dst_ref=v_from[1 << bit].at[chunk],
                send_sem=g_send.at[1 << bit], recv_sem=g_recv.at[1 << bit],
                device_id=(me_k, flipped(me_g, bit)), device_id_type=MESH,
            ).start()

    def whole_block(offset, bit):
        return pltpu.make_async_remote_copy(
            src_ref=v_from[offset], dst_ref=v_from[offset | (1 << bit)],
            send_sem=g_send.at[offset | (1 << bit)], recv_sem=g_recv.at[offset | (1 << bit)],
            device_id=(me_k, flipped(me_g, bit)), device_id_type=MESH,
        )

    def c_step(step):
        from_left, from_right = ring_member(place - step, n_k), ring_member(place + step, n_k)
        c_copy(from_left, 0, right).wait_recv()
        if step < n_right:
            c_copy(from_left, step, right).start()
        if step <= n_left:
            c_copy(from_right, 0, left).wait_recv()
            if step < n_left:
                c_copy(from_right, n_right + step, left).start()

    def v_step(step):
        from_left, from_right = ring_member(place - step, n_k), ring_member(place + step, n_k)
        v_copy(from_left, 0, right).wait_recv()
        if step < n_right:
            v_copy(from_left, step, right).start()
        if step <= n_left:
            v_copy(from_right, 0, left).wait_recv()
            if step < n_left:
                v_copy(from_right, n_right + step, left).start()
            across(from_right)
        across(from_left)

    c_copy(me_k, 0, right).start()
    c_copy(me_k, n_right, left).start()
    v_copy(me_k, 0, right).start()
    v_copy(me_k, n_right, left).start()
    across(me_k)
    for step in range(1, n_right + 1):
        c_step(step)
        if step > 1:
            v_step(step - 1)

    shift = jnp.int32(0)
    for row in range(n_k):
        shift = jnp.where(qtable[row, 0] == me_k, row, shift)

    def build(k, carry):
        partner = lax.rem(k - shift + n_k, n_k)
        dens = densities(c_all[k][:n_c], c_all[partner][n_c:])
        pc[pl.ds(pl.multiple_of(k * rows, rows), rows), :] = dens
        return carry

    lax.fori_loop(0, n_k, build, 0)
    tiles[...] = jnp.zeros_like(tiles)

    sub = min(512, width)
    unit = 8
    group = 4
    cuts = width // sub

    def work(weigh, close):
        if weigh is not None:
            block = moved(me_g, weigh, bits)
            loads[weigh].wait()

        def step(number, carry):
            which, column = number // cuts, number % cuts
            columns = pl.ds(pl.multiple_of(column * sub, sub), sub)
            all_rows = pl.ds(pl.multiple_of(which * (unit * rows), unit * rows), unit * rows)
            if weigh is not None:
                w_from[weigh][all_rows, columns] = jnp.dot(
                    pc[all_rows, :], s_held[block, :, columns], preferred_element_type=F32
                ).astype(BF16)
            if close is not None:
                for part in range(unit // group):
                    dens = []
                    for k in range(group):
                        k = which * unit + part * group + k
                        partner = lax.rem(k - shift + n_k, n_k)
                        own = v_from[close][k, :, columns][:n_c]
                        far = v_from[close][partner, :, columns][n_c:]
                        dens.append(densities(own, far))
                    first = pl.multiple_of((which * unit + part * group) * rows, group * rows)
                    tiles[which * (unit // group) + part] += lax.dot_general(
                        w_from[close][pl.ds(first, group * rows), columns],
                        jnp.concatenate(dens, axis=0),
                        (((1,), (1,)), ((), ())),
                        preferred_element_type=F32,
                    )
            return carry

        lax.fori_loop(0, (n_k // unit) * cuts, step, 0)

    def pass_on(offset):
        if offset == 0:
            return
        low = (offset & -offset).bit_length() - 1
        whole_block(offset & (offset - 1), low).wait_recv()
        for bit in reversed(range(low)):
            whole_block(offset, bit).start()

    order = sorted(range(n_g), key=lambda offset: (bin(offset).count("1"), -offset))
    work(order[0], None)
    v_step(n_right)
    work(order[1], None)
    for number in range(2, n_g):
        pass_on(order[number - 1])
        work(order[number], order[number - 2])
    for offset in order[n_g - 2 :]:
        if offset == order[-1]:
            pass_on(offset)
        work(None, offset)

    share = rows // n_g
    half = share // 2

    def lay_out(which, carry):
        for k in range(group):
            for to in range(n_g):
                first = k * rows + to * share
                lanes = slice(k * rows, (k + 1) * rows)
                sent[to, which * group + k] = jnp.concatenate(
                    [
                        tiles[which, first : first + half, lanes],
                        tiles[which, first + half : first + share, lanes],
                    ],
                    axis=1,
                )
        return carry

    lax.fori_loop(0, n_k // group, lay_out, 0)

    partials = []
    for offset in reversed(range(1, n_g)):
        to = moved(me_g, offset, bits)
        partial = pltpu.make_async_remote_copy(
            src_ref=sent.at[to], dst_ref=got.at[offset],
            send_sem=p_send.at[offset], recv_sem=p_recv.at[offset],
            device_id=(me_k, to), device_id_type=MESH,
        )
        partial.start()
        partials.append(partial)

    for slot in range(n_k - 1):
        c_copy(me_k, slot, right).wait_send()
        v_copy(me_k, slot, right).wait_send()
    for offset in range(1, n_g):
        low = (offset & -offset).bit_length() - 1
        whole_block(offset & (offset - 1), low).wait_send()

    for partial in partials:
        partial.wait_recv()
    value = sent[me_g]
    for offset in range(1, n_g):
        value += got[offset]
    summed[...] = value

    def hand_out(step, carry):
        peer = (me_k + step) % n_k
        pltpu.make_async_remote_copy(
            src_ref=summed.at[peer], dst_ref=came.at[me_k],
            send_sem=t_send, recv_sem=t_recv,
            device_id=(peer, me_g), device_id_type=MESH,
        ).start()
        return carry

    lax.fori_loop(1, n_k, hand_out, 0)
    came[me_k] = summed[me_k]
    for partial in partials:
        partial.wait_send()

    handed = pltpu.make_async_remote_copy(
        src_ref=summed.at[pl.ds(0, n_k - 1)], dst_ref=came.at[pl.ds(0, n_k - 1)],
        send_sem=t_send, recv_sem=t_recv,
        device_id=(right, me_g), device_id_type=MESH,
    )
    handed.wait_recv()
    for number in range(NSHIFT + 1):
        value = came[qtable[number, 0]]
        out[number, :half, :] = value[:, :rows]
        out[number, half:, :] = value[:, rows:]
    handed.wait_send()


def per_device(cond, vale, screen, qtable, gmap):
    n_k, n_g = lax.axis_size("ka"), lax.axis_size("ga")
    n_c, width = cond.shape[1], cond.shape[2]
    rows = n_c * n_c
    share = rows // n_g
    anywhere = pl.BlockSpec(memory_space=pltpu.HBM)
    dma = pltpu.SemaphoreType.DMA
    result = pl.pallas_call(
        functools.partial(kernel, n_k, n_g),
        out_shape=jax.ShapeDtypeStruct((NSHIFT + 1, share, rows), F32),
        in_specs=[anywhere] * 5,
        out_specs=pl.BlockSpec(memory_space=pltpu.VMEM),
        scratch_shapes=[
            pltpu.VMEM(cond.shape, BF16),
            pltpu.VMEM(vale.shape, BF16),
            pltpu.SMEM(qtable.shape, jnp.int32),
            pltpu.VMEM(gmap.shape, jnp.int32),
            pltpu.VMEM((n_g, width, width), BF16),
            pltpu.VMEM((n_k, 2 * n_c, width), BF16),
            pltpu.VMEM((n_k * rows, width), BF16),
            pltpu.VMEM((n_k // 4, 4 * rows, 4 * rows), F32),
            pltpu.VMEM((n_g, n_k, share // 2, 2 * rows), F32),
            pltpu.VMEM((n_g, n_k, share // 2, 2 * rows), F32),
            pltpu.VMEM((n_k, share // 2, 2 * rows), F32),
            pltpu.VMEM((n_k, share // 2, 2 * rows), F32),
            dma((4,)), dma((n_g,)), dma((n_k,)), dma((n_k,)), dma((n_k,)), dma((n_k,)),
            dma((n_g,)), dma((n_g,)), dma((n_g,)), dma((n_g,)), dma(()), dma(()),
        ]
        + [pltpu.VMEM((n_k, 2 * n_c, width), BF16)] * n_g
        + [pltpu.VMEM((n_k * rows, width), BF16)] * n_g,
        compiler_params=pltpu.CompilerParams(
            collective_id=0, has_side_effects=True, vmem_limit_bytes=63 * 1024 * 1024
        ),
        cost_estimate=pl.CostEstimate(
            flops=2 * n_k * rows * width * screen.shape[2],
            bytes_accessed=2 * width * screen.shape[2],
            transcendentals=0,
        ),
    )(cond, vale, screen, qtable, gmap)
    return result.reshape(1, NSHIFT + 1, share * rows)


def solution(mesh):
    in_specs = (P("ka", None, "ga"), P("ka", None, "ga"), P("ka", "ga", None), P(), P("ka", "ga"))
    out_specs = P("ka", None, "ga")
    return jax.shard_map(
        per_device, mesh=mesh, in_specs=in_specs, out_specs=out_specs, check_vma=False
    )
```

```python
import functools

import jax
import jax.numpy as jnp
from jax import lax
from jax.experimental import pallas as pl
from jax.experimental.pallas import tpu as pltpu
from jax.sharding import PartitionSpec as P

NSHIFT = 2
MESH = pl.DeviceIdType.MESH
F32 = jnp.float32
BF16 = jnp.bfloat16


def flipped(index, bit):
    width = 1 << bit
    return index + width * (1 - 2 * ((index // width) % 2))


def moved(index, offset, bits):
    for bit in range(bits):
        if (offset >> bit) & 1:
            index = flipped(index, bit)
    return index


def densities(own, far):
    product = own.astype(F32)[:, None, :] * far.astype(F32)[None, :, :]
    return product.reshape(-1, own.shape[-1]).astype(BF16)


def kernel(
    n_k, n_g, cond_in, vale_in, screen, qtable_in, gmap_in, out,
    cond, vale, qtable, gmap, s_held, c_all, pc, tiles, sent, got,
    in_sem, s_sem, c_send, c_recv, v_send, v_recv, g_send, g_recv,
    t_send, t_recv, *blocks,
):
    v_from, w_from = blocks[:n_g], blocks[n_g:]
    bits = n_g.bit_length() - 1
    width = cond.shape[2]
    n_c = cond.shape[1]
    rows = n_c * n_c
    total = n_k * n_g
    me_k, me_g = lax.axis_index("ka"), lax.axis_index("ga")
    me = me_k * n_g + me_g

    arrivals = [
        pltpu.make_async_copy(source, target, in_sem.at[number])
        for number, (source, target) in enumerate(
            [(gmap_in, gmap), (cond_in, cond), (vale_in, vale), (qtable_in, qtable)]
        )
    ]
    for arrival in arrivals:
        arrival.start()

    barrier = pltpu.get_barrier_semaphore()

    def greet(step, carry):
        peer = (me + step) % total
        pl.semaphore_signal(
            barrier, inc=1, device_id=(peer // n_g, peer % n_g), device_id_type=MESH
        )
        return carry

    lax.fori_loop(1, total, greet, 0)

    loads = []
    for offset in range(n_g):
        block = moved(me_g, offset, bits)
        load = pltpu.make_async_copy(
            screen.at[0, :, pl.ds(pl.multiple_of(block * width, width), width)],
            s_held.at[block],
            s_sem.at[offset],
        )
        load.start()
        loads.append(load)

    for arrival in arrivals:
        arrival.wait()

    local_map = gmap[...] - me_g * width
    both = jnp.concatenate([cond[0], vale[0]], axis=0)
    part = min(256, width)
    mapped = jnp.zeros((2 * n_c, width), F32)
    for first in range(0, width, part):
        points = lax.broadcasted_iota(jnp.int32, (part, width), 0) + first
        pick = jnp.where(points == local_map, 1.0, 0.0).astype(BF16)
        mapped += jnp.dot(both[:, first : first + part], pick, preferred_element_type=F32)
    mapped = mapped.astype(BF16)
    c_all[me_k] = jnp.concatenate([cond[0], mapped[:n_c]], axis=0)
    v_from[0][me_k] = jnp.concatenate([vale[0], mapped[n_c:]], axis=0)

    pl.semaphore_wait(barrier, total - 1)

    depth = n_k // 2
    me_z, me_y = me_k // 2, me_k % 2
    other = me_z * 2 + 1 - me_y

    def along(step):
        return ((me_z + step) % depth) * 2 + me_y

    def beside(step):
        return ((me_z + step) % depth) * 2 + 1 - me_y

    def c_copy(chunk, slot, target):
        return pltpu.make_async_remote_copy(
            src_ref=c_all.at[chunk], dst_ref=c_all.at[chunk],
            send_sem=c_send.at[slot], recv_sem=c_recv.at[chunk],
            device_id=(target, me_g), device_id_type=MESH,
        )

    def v_copy(chunk, slot, target):
        return pltpu.make_async_remote_copy(
            src_ref=v_from[0].at[chunk], dst_ref=v_from[0].at[chunk],
            send_sem=v_send.at[slot], recv_sem=v_recv.at[chunk],
            device_id=(target, me_g), device_id_type=MESH,
        )

    def across(chunk):
        for bit in reversed(range(bits)):
            pltpu.make_async_remote_copy(
                src_ref=v_from[0].at[chunk], dst_ref=v_from[1 << bit].at[chunk],
                send_sem=g_send.at[1 << bit], recv_sem=g_recv.at[1 << bit],
                device_id=(me_k, flipped(me_g, bit)), device_id_type=MESH,
            ).start()

    def whole_block(offset, bit):
        return pltpu.make_async_remote_copy(
            src_ref=v_from[offset], dst_ref=v_from[offset | (1 << bit)],
            send_sem=g_send.at[offset | (1 << bit)], recv_sem=g_recv.at[offset | (1 << bit)],
            device_id=(me_k, flipped(me_g, bit)), device_id_type=MESH,
        )

    for copy in (c_copy, v_copy):
        for step in range(1, depth):
            copy(me_k, step - 1, along(step)).start()
        copy(me_k, depth - 1, other).start()
    across(me_k)
    for step in range(1, depth):
        c_copy(along(step), 0, other).wait_recv()
        c_copy(along(step), depth - 1 + step, other).start()
    for step in range(1, depth):
        v_copy(along(step), 0, other).wait_recv()
        v_copy(along(step), depth - 1 + step, other).start()
        across(along(step))
    for step in range(depth):
        c_copy(beside(step), 0, other).wait_recv()

    shift = jnp.int32(0)
    for row in range(n_k):
        shift = jnp.where(qtable[row, 0] == me_k, row, shift)

    def build(k, carry):
        partner = lax.rem(k - shift + n_k, n_k)
        dens = densities(c_all[k][:n_c], c_all[partner][n_c:])
        pc[pl.ds(pl.multiple_of(k * rows, rows), rows), :] = dens
        return carry

    lax.fori_loop(0, n_k, build, 0)
    tiles[...] = jnp.zeros_like(tiles)

    sub = min(512, width)
    unit = 8
    group = 4
    cuts = width // sub

    def work(weigh, close):
        if weigh is not None:
            block = moved(me_g, weigh, bits)
            loads[weigh].wait()

        def step(number, carry):
            which, column = number // cuts, number % cuts
            columns = pl.ds(pl.multiple_of(column * sub, sub), sub)
            all_rows = pl.ds(pl.multiple_of(which * (unit * rows), unit * rows), unit * rows)
            if weigh is not None:
                w_from[weigh][all_rows, columns] = jnp.dot(
                    pc[all_rows, :], s_held[block, :, columns], preferred_element_type=F32
                ).astype(BF16)
            if close is not None:
                for part in range(unit // group):
                    dens = []
                    for k in range(group):
                        k = which * unit + part * group + k
                        partner = lax.rem(k - shift + n_k, n_k)
                        own = v_from[close][k, :, columns][:n_c]
                        far = v_from[close][partner, :, columns][n_c:]
                        dens.append(densities(own, far))
                    first = pl.multiple_of((which * unit + part * group) * rows, group * rows)
                    tiles[which * (unit // group) + part] += lax.dot_general(
                        w_from[close][pl.ds(first, group * rows), columns],
                        jnp.concatenate(dens, axis=0),
                        (((1,), (1,)), ((), ())),
                        preferred_element_type=F32,
                    )
            return carry

        lax.fori_loop(0, (n_k // unit) * cuts, step, 0)

    def pass_on(offset):
        if offset == 0:
            return
        low = (offset & -offset).bit_length() - 1
        whole_block(offset & (offset - 1), low).wait_recv()
        for bit in reversed(range(low)):
            whole_block(offset, bit).start()

    order = sorted(range(n_g), key=lambda offset: (bin(offset).count("1"), -offset))
    work(order[0], None)
    for step in range(depth):
        v_copy(beside(step), 0, other).wait_recv()
        across(beside(step))
    work(order[1], None)
    for number in range(2, n_g):
        pass_on(order[number - 1])
        work(order[number], order[number - 2])
    for offset in order[n_g - 2 :]:
        if offset == order[-1]:
            pass_on(offset)
        work(None, offset)

    share = rows // n_g
    half = share // 2

    def lay_out(which, carry):
        for k in range(group):
            for to in range(n_g):
                first = k * rows + to * share
                lanes = slice(k * rows, (k + 1) * rows)
                sent[(which * group + k) * n_g + to] = jnp.concatenate(
                    [
                        tiles[which, first : first + half, lanes],
                        tiles[which, first + half : first + share, lanes],
                    ],
                    axis=1,
                )
        return carry

    lax.fori_loop(0, n_k // group, lay_out, 0)

    def hand_out(step, carry):
        peer = (me + step) % total
        pltpu.make_async_remote_copy(
            src_ref=sent.at[peer], dst_ref=got.at[me],
            send_sem=t_send, recv_sem=t_recv,
            device_id=(peer // n_g, peer % n_g), device_id_type=MESH,
        ).start()
        return carry

    lax.fori_loop(1, total, hand_out, 0)
    got[me] = sent[me]

    for slot in range(n_k - 1):
        c_copy(me_k, slot, other).wait_send()
        v_copy(me_k, slot, other).wait_send()
    for offset in range(1, n_g):
        low = (offset & -offset).bit_length() - 1
        whole_block(offset & (offset - 1), low).wait_send()

    handed = pltpu.make_async_remote_copy(
        src_ref=sent.at[pl.ds(0, total - 1)], dst_ref=got.at[pl.ds(0, total - 1)],
        send_sem=t_send, recv_sem=t_recv,
        device_id=(other, me_g), device_id_type=MESH,
    )
    handed.wait_recv()
    for number in range(NSHIFT + 1):
        holder = qtable[number, 0]
        value = got[holder * n_g]
        for source in range(1, n_g):
            value += got[holder * n_g + source]
        out[number, :half, :] = value[:, :rows]
        out[number, half:, :] = value[:, rows:]
    handed.wait_send()


def per_device(cond, vale, screen, qtable, gmap):
    n_k, n_g = lax.axis_size("ka"), lax.axis_size("ga")
    n_c, width = cond.shape[1], cond.shape[2]
    rows = n_c * n_c
    share = rows // n_g
    total = n_k * n_g
    anywhere = pl.BlockSpec(memory_space=pltpu.HBM)
    dma = pltpu.SemaphoreType.DMA
    result = pl.pallas_call(
        functools.partial(kernel, n_k, n_g),
        out_shape=jax.ShapeDtypeStruct((NSHIFT + 1, share, rows), F32),
        in_specs=[anywhere] * 5,
        out_specs=pl.BlockSpec(memory_space=pltpu.VMEM),
        scratch_shapes=[
            pltpu.VMEM(cond.shape, BF16),
            pltpu.VMEM(vale.shape, BF16),
            pltpu.SMEM(qtable.shape, jnp.int32),
            pltpu.VMEM(gmap.shape, jnp.int32),
            pltpu.VMEM((n_g, width, width), BF16),
            pltpu.VMEM((n_k, 2 * n_c, width), BF16),
            pltpu.VMEM((n_k * rows, width), BF16),
            pltpu.VMEM((n_k // 4, 4 * rows, 4 * rows), F32),
            pltpu.VMEM((total, share // 2, 2 * rows), F32),
            pltpu.VMEM((total, share // 2, 2 * rows), F32),
            dma((4,)), dma((n_g,)), dma((n_k,)), dma((n_k,)), dma((n_k,)), dma((n_k,)),
            dma((n_g,)), dma((n_g,)), dma(()), dma(()),
        ]
        + [pltpu.VMEM((n_k, 2 * n_c, width), BF16)] * n_g
        + [pltpu.VMEM((n_k * rows, width), BF16)] * n_g,
        compiler_params=pltpu.CompilerParams(
            collective_id=0, has_side_effects=True, vmem_limit_bytes=63 * 1024 * 1024
        ),
        cost_estimate=pl.CostEstimate(
            flops=2 * n_k * rows * width * screen.shape[2],
            bytes_accessed=2 * width * screen.shape[2],
            transcendentals=0,
        ),
    )(cond, vale, screen, qtable, gmap)
    return result.reshape(1, NSHIFT + 1, share * rows)


def solution(mesh):
    in_specs = (P("ka", None, "ga"), P("ka", None, "ga"), P("ka", "ga", None), P(), P("ka", "ga"))
    out_specs = P("ka", None, "ga")
    return jax.shard_map(
        per_device, mesh=mesh, in_specs=in_specs, out_specs=out_specs, check_vma=False
    )
```

```python
import functools

import jax
import jax.numpy as jnp
from jax import lax
from jax.experimental import pallas as pl
from jax.experimental.pallas import tpu as pltpu
from jax.sharding import PartitionSpec as P

NSHIFT = 2
MESH = pl.DeviceIdType.MESH
F32 = jnp.float32
BF16 = jnp.bfloat16


def flipped(index, bit):
    width = 1 << bit
    return index + width * (1 - 2 * ((index // width) % 2))


def moved(index, offset, bits):
    for bit in range(bits):
        if (offset >> bit) & 1:
            index = flipped(index, bit)
    return index


def densities(own, far):
    product = own.astype(F32)[:, None, :] * far.astype(F32)[None, :, :]
    return product.reshape(-1, own.shape[-1]).astype(BF16)


def kernel(
    n_k, n_g, cond_in, vale_in, screen, qtable_in, gmap_in, out,
    cond, vale, qtable, gmap, s_held, c_all, pc, tiles, sent, got,
    in_sem, s_sem, c_send, c_recv, v_send, v_recv, g_send, g_recv,
    t_send, t_recv, *blocks,
):
    v_from, w_from = blocks[:n_g], blocks[n_g:]
    bits = n_g.bit_length() - 1
    width = cond.shape[2]
    n_c = cond.shape[1]
    rows = n_c * n_c
    total = n_k * n_g
    me_k, me_g = lax.axis_index("ka"), lax.axis_index("ga")
    me = me_k * n_g + me_g

    arrivals = [
        pltpu.make_async_copy(source, target, in_sem.at[number])
        for number, (source, target) in enumerate(
            [(gmap_in, gmap), (cond_in, cond), (vale_in, vale), (qtable_in, qtable)]
        )
    ]
    for arrival in arrivals:
        arrival.start()

    barrier = pltpu.get_barrier_semaphore()

    def greet(step, carry):
        peer = (me + step) % total
        pl.semaphore_signal(
            barrier, inc=1, device_id=(peer // n_g, peer % n_g), device_id_type=MESH
        )
        return carry

    lax.fori_loop(1, total, greet, 0)

    loads = []
    for offset in range(n_g):
        block = moved(me_g, offset, bits)
        load = pltpu.make_async_copy(
            screen.at[0, :, pl.ds(pl.multiple_of(block * width, width), width)],
            s_held.at[block],
            s_sem.at[offset],
        )
        load.start()
        loads.append(load)

    for arrival in arrivals:
        arrival.wait()

    local_map = gmap[...] - me_g * width
    both = jnp.concatenate([cond[0], vale[0]], axis=0)
    lanes = min(128, width)
    points = lax.broadcasted_iota(jnp.int32, (lanes, width), 0)
    pick = jnp.where(points == local_map % lanes, 1.0, 0.0).astype(BF16)
    stacked = jnp.concatenate(
        [both[:, first : first + lanes] for first in range(0, width, lanes)], axis=0
    )
    spread = jnp.dot(stacked, pick, preferred_element_type=F32)
    mapped = jnp.zeros((2 * n_c, width), F32)
    for number in range(width // lanes):
        piece = spread[number * 2 * n_c : (number + 1) * 2 * n_c]
        mapped = jnp.where(local_map // lanes == number, piece, mapped)
    mapped = mapped.astype(BF16)
    c_all[me_k] = jnp.concatenate([cond[0], mapped[:n_c]], axis=0)
    v_from[0][me_k] = jnp.concatenate([vale[0], mapped[n_c:]], axis=0)

    pl.semaphore_wait(barrier, total - 1)

    depth = n_k // 2
    me_z, me_y = me_k // 2, me_k % 2
    other = me_z * 2 + 1 - me_y

    def along(step):
        return ((me_z + step) % depth) * 2 + me_y

    def beside(step):
        return ((me_z + step) % depth) * 2 + 1 - me_y

    def c_copy(chunk, slot, target):
        return pltpu.make_async_remote_copy(
            src_ref=c_all.at[chunk], dst_ref=c_all.at[chunk],
            send_sem=c_send.at[slot], recv_sem=c_recv.at[chunk],
            device_id=(target, me_g), device_id_type=MESH,
        )

    def v_copy(chunk, slot, target):
        return pltpu.make_async_remote_copy(
            src_ref=v_from[0].at[chunk], dst_ref=v_from[0].at[chunk],
            send_sem=v_send.at[slot], recv_sem=v_recv.at[chunk],
            device_id=(target, me_g), device_id_type=MESH,
        )

    def across(chunk):
        for bit in reversed(range(bits)):
            pltpu.make_async_remote_copy(
                src_ref=v_from[0].at[chunk], dst_ref=v_from[1 << bit].at[chunk],
                send_sem=g_send.at[1 << bit], recv_sem=g_recv.at[1 << bit],
                device_id=(me_k, flipped(me_g, bit)), device_id_type=MESH,
            ).start()

    def whole_block(offset, bit):
        return pltpu.make_async_remote_copy(
            src_ref=v_from[offset], dst_ref=v_from[offset | (1 << bit)],
            send_sem=g_send.at[offset | (1 << bit)], recv_sem=g_recv.at[offset | (1 << bit)],
            device_id=(me_k, flipped(me_g, bit)), device_id_type=MESH,
        )

    for step in range(1, depth):
        c_copy(me_k, step - 1, along(step)).start()
    c_copy(me_k, depth - 1, other).start()
    across(me_k)
    for step in range(1, depth):
        c_copy(along(step), 0, other).wait_recv()
        c_copy(along(step), depth - 1 + step, other).start()
    for step in range(1, depth):
        v_copy(me_k, step - 1, along(step)).start()
    v_copy(me_k, depth - 1, other).start()
    for step in range(depth):
        c_copy(beside(step), 0, other).wait_recv()

    shift = jnp.int32(0)
    for row in range(n_k):
        shift = jnp.where(qtable[row, 0] == me_k, row, shift)

    def build(k, carry):
        partner = lax.rem(k - shift + n_k, n_k)
        dens = densities(c_all[k][:n_c], c_all[partner][n_c:])
        pc[pl.ds(pl.multiple_of(k * rows, rows), rows), :] = dens
        return carry

    lax.fori_loop(0, n_k, build, 0)
    tiles[...] = jnp.zeros_like(tiles)

    sub = min(512, width)
    unit = 8
    group = 4
    cuts = width // sub

    def work(weigh, close):
        if weigh is not None:
            block = moved(me_g, weigh, bits)
            loads[weigh].wait()

        def step(number, carry):
            which, column = number // cuts, number % cuts
            columns = pl.ds(pl.multiple_of(column * sub, sub), sub)
            all_rows = pl.ds(pl.multiple_of(which * (unit * rows), unit * rows), unit * rows)
            if weigh is not None:
                w_from[weigh][all_rows, columns] = jnp.dot(
                    pc[all_rows, :], s_held[block, :, columns], preferred_element_type=F32
                ).astype(BF16)
            if close is not None:
                for part in range(unit // group):
                    dens = []
                    for k in range(group):
                        k = which * unit + part * group + k
                        partner = lax.rem(k - shift + n_k, n_k)
                        own = v_from[close][k, :, columns][:n_c]
                        far = v_from[close][partner, :, columns][n_c:]
                        dens.append(densities(own, far))
                    first = pl.multiple_of((which * unit + part * group) * rows, group * rows)
                    tiles[which * (unit // group) + part] += lax.dot_general(
                        w_from[close][pl.ds(first, group * rows), columns],
                        jnp.concatenate(dens, axis=0),
                        (((1,), (1,)), ((), ())),
                        preferred_element_type=F32,
                    )
            return carry

        lax.fori_loop(0, (n_k // unit) * cuts, step, 0)

    passed = {0}

    def pass_on(offset):
        if offset in passed:
            return
        passed.add(offset)
        low = (offset & -offset).bit_length() - 1
        whole_block(offset & (offset - 1), low).wait_recv()
        for bit in reversed(range(low)):
            whole_block(offset, bit).start()

    order = sorted(range(n_g), key=lambda offset: (bin(offset).count("1"), offset))
    work(order[0], None)
    for step in range(1, depth):
        v_copy(along(step), 0, other).wait_recv()
        v_copy(along(step), depth - 1 + step, other).start()
        across(along(step))
    work(order[1], None)
    for step in range(depth):
        v_copy(beside(step), 0, other).wait_recv()
        across(beside(step))
    for number in range(2, n_g):
        if number > 2:
            pass_on(order[number - 2])
            pass_on(order[number - 1])
        work(order[number], order[number - 2])
    for offset in order[n_g - 2 :]:
        pass_on(offset)
        work(None, offset)

    share = rows // n_g
    half = share // 2

    def lay_out(which, carry):
        for k in range(group):
            for to in range(n_g):
                first = k * rows + to * share
                lanes = slice(k * rows, (k + 1) * rows)
                sent[(which * group + k) * n_g + to] = jnp.concatenate(
                    [
                        tiles[which, first : first + half, lanes],
                        tiles[which, first + half : first + share, lanes],
                    ],
                    axis=1,
                )
        return carry

    lax.fori_loop(0, n_k // group, lay_out, 0)

    def hand_out(step, carry):
        peer = (me + step) % total
        pltpu.make_async_remote_copy(
            src_ref=sent.at[peer], dst_ref=got.at[me],
            send_sem=t_send, recv_sem=t_recv,
            device_id=(peer // n_g, peer % n_g), device_id_type=MESH,
        ).start()
        return carry

    lax.fori_loop(1, total, hand_out, 0)
    got[me] = sent[me]

    for slot in range(n_k - 1):
        c_copy(me_k, slot, other).wait_send()
        v_copy(me_k, slot, other).wait_send()
    for offset in range(1, n_g):
        low = (offset & -offset).bit_length() - 1
        whole_block(offset & (offset - 1), low).wait_send()

    handed = pltpu.make_async_remote_copy(
        src_ref=sent.at[pl.ds(0, total - 1)], dst_ref=got.at[pl.ds(0, total - 1)],
        send_sem=t_send, recv_sem=t_recv,
        device_id=(other, me_g), device_id_type=MESH,
    )
    handed.wait_recv()
    for number in range(NSHIFT + 1):
        holder = qtable[number, 0]
        value = got[holder * n_g]
        for source in range(1, n_g):
            value += got[holder * n_g + source]
        for row in range(share):
            side = row // half
            first = row - side * half
            out[0, number : number + 1, row * rows : (row + 1) * rows] = value[
                first : first + 1, side * rows : (side + 1) * rows
            ]
    handed.wait_send()


def per_device(cond, vale, screen, qtable, gmap):
    n_k, n_g = lax.axis_size("ka"), lax.axis_size("ga")
    n_c, width = cond.shape[1], cond.shape[2]
    rows = n_c * n_c
    share = rows // n_g
    total = n_k * n_g
    anywhere = pl.BlockSpec(memory_space=pltpu.HBM)
    dma = pltpu.SemaphoreType.DMA
    return pl.pallas_call(
        functools.partial(kernel, n_k, n_g),
        out_shape=jax.ShapeDtypeStruct((1, NSHIFT + 1, share * rows), F32),
        in_specs=[anywhere] * 5,
        out_specs=pl.BlockSpec(memory_space=pltpu.VMEM),
        scratch_shapes=[
            pltpu.VMEM(cond.shape, BF16),
            pltpu.VMEM(vale.shape, BF16),
            pltpu.SMEM(qtable.shape, jnp.int32),
            pltpu.VMEM(gmap.shape, jnp.int32),
            pltpu.VMEM((n_g, width, width), BF16),
            pltpu.VMEM((n_k, 2 * n_c, width), BF16),
            pltpu.VMEM((n_k * rows, width), BF16),
            pltpu.VMEM((n_k // 4, 4 * rows, 4 * rows), F32),
            pltpu.VMEM((total, share // 2, 2 * rows), F32),
            pltpu.VMEM((total, share // 2, 2 * rows), F32),
            dma((4,)), dma((n_g,)), dma((n_k,)), dma((n_k,)), dma((n_k,)), dma((n_k,)),
            dma((n_g,)), dma((n_g,)), dma(()), dma(()),
        ]
        + [pltpu.VMEM((n_k, 2 * n_c, width), BF16)] * n_g
        + [pltpu.VMEM((n_k * rows, width), BF16)] * n_g,
        compiler_params=pltpu.CompilerParams(
            collective_id=0, has_side_effects=True, vmem_limit_bytes=63 * 1024 * 1024
        ),
        cost_estimate=pl.CostEstimate(
            flops=2 * n_k * rows * width * screen.shape[2],
            bytes_accessed=2 * width * screen.shape[2],
            transcendentals=0,
        ),
    )(cond, vale, screen, qtable, gmap)


def solution(mesh):
    in_specs = (P("ka", None, "ga"), P("ka", None, "ga"), P("ka", "ga", None), P(), P("ka", "ga"))
    out_specs = P("ka", None, "ga")
    return jax.shard_map(
        per_device, mesh=mesh, in_specs=in_specs, out_specs=out_specs, check_vma=False
    )
```

```python
import functools

import jax
import jax.numpy as jnp
from jax import lax
from jax.experimental import pallas as pl
from jax.experimental.pallas import tpu as pltpu
from jax.sharding import PartitionSpec as P

NSHIFT = 2
MESH = pl.DeviceIdType.MESH
F32 = jnp.float32
BF16 = jnp.bfloat16


def flipped(index, bit):
    width = 1 << bit
    return index + width * (1 - 2 * ((index // width) % 2))


def moved(index, offset, bits):
    for bit in range(bits):
        if (offset >> bit) & 1:
            index = flipped(index, bit)
    return index


def densities(own, far):
    product = own.astype(F32)[:, None, :] * far.astype(F32)[None, :, :]
    return product.reshape(-1, own.shape[-1]).astype(BF16)


def kernel(
    n_k, n_g, cond_in, vale_in, screen, qtable_in, gmap_in, out,
    cond, vale, qtable, gmap, s_held, c_all, pc, tiles, sent, got,
    in_sem, s_sem, c_send, c_recv, v_send, v_recv, g_send, g_recv,
    t_send, t_recv, *blocks,
):
    v_from, w_from = blocks[:n_g], blocks[n_g:]
    bits = n_g.bit_length() - 1
    width = cond.shape[2]
    n_c = cond.shape[1]
    rows = n_c * n_c
    total = n_k * n_g
    me_k, me_g = lax.axis_index("ka"), lax.axis_index("ga")
    me = me_k * n_g + me_g

    arrivals = [
        pltpu.make_async_copy(source, target, in_sem.at[number])
        for number, (source, target) in enumerate(
            [(gmap_in, gmap), (cond_in, cond), (vale_in, vale), (qtable_in, qtable)]
        )
    ]
    for arrival in arrivals:
        arrival.start()

    depth = n_k // 2
    me_z, me_y = me_k // 2, me_k % 2
    other = me_z * 2 + 1 - me_y

    def along(step):
        return ((me_z + step) % depth) * 2 + me_y

    def beside(step):
        return ((me_z + step) % depth) * 2 + 1 - me_y

    barrier = pltpu.get_barrier_semaphore()
    peers = [(along(step), me_g) for step in range(1, depth)] + [(other, me_g)]
    peers += [(me_k, flipped(me_g, bit)) for bit in range(bits)]
    for peer in peers:
        pl.semaphore_signal(barrier, inc=1, device_id=peer, device_id_type=MESH)

    loads = []
    for offset in range(n_g):
        block = moved(me_g, offset, bits)
        load = pltpu.make_async_copy(
            screen.at[0, :, pl.ds(pl.multiple_of(block * width, width), width)],
            s_held.at[block],
            s_sem.at[offset],
        )
        load.start()
        loads.append(load)

    for arrival in arrivals:
        arrival.wait()

    local_map = gmap[...] - me_g * width
    both = jnp.concatenate([cond[0], vale[0]], axis=0)
    lanes = min(128, width)
    points = lax.broadcasted_iota(jnp.int32, (lanes, width), 0)
    pick = jnp.where(points == local_map % lanes, 1.0, 0.0).astype(BF16)
    stacked = jnp.concatenate(
        [both[:, first : first + lanes] for first in range(0, width, lanes)], axis=0
    )
    spread = jnp.dot(stacked, pick, preferred_element_type=F32)
    mapped = jnp.zeros((2 * n_c, width), F32)
    for number in range(width // lanes):
        piece = spread[number * 2 * n_c : (number + 1) * 2 * n_c]
        mapped = jnp.where(local_map // lanes == number, piece, mapped)
    mapped = mapped.astype(BF16)
    c_all[me_k] = jnp.concatenate([cond[0], mapped[:n_c]], axis=0)
    v_from[0][me_k] = jnp.concatenate([vale[0], mapped[n_c:]], axis=0)

    pl.semaphore_wait(barrier, len(peers))

    def c_copy(chunk, slot, target):
        return pltpu.make_async_remote_copy(
            src_ref=c_all.at[chunk], dst_ref=c_all.at[chunk],
            send_sem=c_send.at[slot], recv_sem=c_recv.at[chunk],
            device_id=(target, me_g), device_id_type=MESH,
        )

    def v_copy(chunk, slot, target):
        return pltpu.make_async_remote_copy(
            src_ref=v_from[0].at[chunk], dst_ref=v_from[0].at[chunk],
            send_sem=v_send.at[slot], recv_sem=v_recv.at[chunk],
            device_id=(target, me_g), device_id_type=MESH,
        )

    def across(chunk):
        for bit in reversed(range(bits)):
            pltpu.make_async_remote_copy(
                src_ref=v_from[0].at[chunk], dst_ref=v_from[1 << bit].at[chunk],
                send_sem=g_send.at[1 << bit], recv_sem=g_recv.at[1 << bit],
                device_id=(me_k, flipped(me_g, bit)), device_id_type=MESH,
            ).start()

    def whole_block(offset, bit):
        return pltpu.make_async_remote_copy(
            src_ref=v_from[offset], dst_ref=v_from[offset | (1 << bit)],
            send_sem=g_send.at[offset | (1 << bit)], recv_sem=g_recv.at[offset | (1 << bit)],
            device_id=(me_k, flipped(me_g, bit)), device_id_type=MESH,
        )

    for step in range(1, depth):
        c_copy(me_k, step - 1, along(step)).start()
    c_copy(me_k, depth - 1, other).start()
    across(me_k)
    for step in range(1, depth):
        c_copy(along(step), 0, other).wait_recv()
        c_copy(along(step), depth - 1 + step, other).start()
    for step in range(1, depth):
        v_copy(me_k, step - 1, along(step)).start()
    v_copy(me_k, depth - 1, other).start()
    for step in range(depth):
        c_copy(beside(step), 0, other).wait_recv()

    shift = jnp.int32(0)
    for row in range(n_k):
        shift = jnp.where(qtable[row, 0] == me_k, row, shift)

    def build(k, carry):
        partner = lax.rem(k - shift + n_k, n_k)
        dens = densities(c_all[k][:n_c], c_all[partner][n_c:])
        pc[pl.ds(pl.multiple_of(k * rows, rows), rows), :] = dens
        return carry

    lax.fori_loop(0, n_k, build, 0)
    tiles[...] = jnp.zeros_like(tiles)

    sub = min(512, width)
    unit = 8
    group = 4
    cuts = width // sub

    def work(weigh, close):
        if weigh is not None:
            block = moved(me_g, weigh, bits)
            loads[weigh].wait()

        def step(number, carry):
            which, column = number // cuts, number % cuts
            columns = pl.ds(pl.multiple_of(column * sub, sub), sub)
            all_rows = pl.ds(pl.multiple_of(which * (unit * rows), unit * rows), unit * rows)
            if weigh is not None:
                w_from[weigh][all_rows, columns] = jnp.dot(
                    pc[all_rows, :], s_held[block, :, columns], preferred_element_type=F32
                ).astype(BF16)
            if close is not None:
                for part in range(unit // group):
                    dens = []
                    for k in range(group):
                        k = which * unit + part * group + k
                        partner = lax.rem(k - shift + n_k, n_k)
                        own = v_from[close][k, :, columns][:n_c]
                        far = v_from[close][partner, :, columns][n_c:]
                        dens.append(densities(own, far))
                    first = pl.multiple_of((which * unit + part * group) * rows, group * rows)
                    tiles[which * (unit // group) + part] += lax.dot_general(
                        w_from[close][pl.ds(first, group * rows), columns],
                        jnp.concatenate(dens, axis=0),
                        (((1,), (1,)), ((), ())),
                        preferred_element_type=F32,
                    )
            return carry

        lax.fori_loop(0, (n_k // unit) * cuts, step, 0)

    passed = {0}

    def pass_on(offset):
        if offset in passed:
            return
        passed.add(offset)
        low = (offset & -offset).bit_length() - 1
        whole_block(offset & (offset - 1), low).wait_recv()
        for bit in reversed(range(low)):
            whole_block(offset, bit).start()

    order = sorted(range(n_g), key=lambda offset: (bin(offset).count("1"), offset))
    work(order[0], None)
    for step in range(1, depth):
        v_copy(along(step), 0, other).wait_recv()
        v_copy(along(step), depth - 1 + step, other).start()
        across(along(step))
    work(order[1], None)
    for step in range(depth):
        v_copy(beside(step), 0, other).wait_recv()
        across(beside(step))
    for number in range(2, n_g):
        if number > 2:
            pass_on(order[number - 2])
            pass_on(order[number - 1])
        work(order[number], order[number - 2])
    for offset in order[n_g - 2 :]:
        pass_on(offset)

    share = rows // n_g
    half = share // 2
    n_groups = n_k // group

    def finish(number, carry):
        which = (me_k // group + number) % n_groups
        tile = tiles[which]
        first = pl.multiple_of(which * (group * rows), group * rows)
        for close in order[n_g - 2 :]:
            for cut in range(cuts):
                columns = slice(cut * sub, (cut + 1) * sub)
                dens = []
                for k in range(group):
                    k = which * group + k
                    partner = lax.rem(k - shift + n_k, n_k)
                    own = v_from[close][k, :, columns][:n_c]
                    far = v_from[close][partner, :, columns][n_c:]
                    dens.append(densities(own, far))
                tile += lax.dot_general(
                    w_from[close][pl.ds(first, group * rows), columns],
                    jnp.concatenate(dens, axis=0),
                    (((1,), (1,)), ((), ())),
                    preferred_element_type=F32,
                )
        for k in range(group):
            for to in range(n_g):
                top = k * rows + to * share
                lanes = slice(k * rows, (k + 1) * rows)
                sent[(which * group + k) * n_g + to] = jnp.concatenate(
                    [tile[top : top + half, lanes], tile[top + half : top + share, lanes]],
                    axis=1,
                )

        def hand_out(step, carry):
            peer = which * (group * n_g) + step

            @pl.when(peer != me)
            def _():
                pltpu.make_async_remote_copy(
                    src_ref=sent.at[peer], dst_ref=got.at[me],
                    send_sem=t_send, recv_sem=t_recv,
                    device_id=(peer // n_g, peer % n_g), device_id_type=MESH,
                ).start()

            return carry

        lax.fori_loop(0, group * n_g, hand_out, 0)
        return carry

    lax.fori_loop(1, n_groups + 1, finish, 0)
    got[me] = sent[me]

    for slot in range(n_k - 1):
        c_copy(me_k, slot, other).wait_send()
        v_copy(me_k, slot, other).wait_send()
    for offset in range(1, n_g):
        low = (offset & -offset).bit_length() - 1
        whole_block(offset & (offset - 1), low).wait_send()

    handed = pltpu.make_async_remote_copy(
        src_ref=sent.at[pl.ds(0, total - 1)], dst_ref=got.at[pl.ds(0, total - 1)],
        send_sem=t_send, recv_sem=t_recv,
        device_id=(other, me_g), device_id_type=MESH,
    )
    handed.wait_recv()
    for number in range(NSHIFT + 1):
        holder = qtable[number, 0]
        value = got[holder * n_g]
        for source in range(1, n_g):
            value += got[holder * n_g + source]
        for row in range(share):
            side = row // half
            first = row - side * half
            out[0, number : number + 1, row * rows : (row + 1) * rows] = value[
                first : first + 1, side * rows : (side + 1) * rows
            ]
    handed.wait_send()


def per_device(cond, vale, screen, qtable, gmap):
    n_k, n_g = lax.axis_size("ka"), lax.axis_size("ga")
    n_c, width = cond.shape[1], cond.shape[2]
    rows = n_c * n_c
    share = rows // n_g
    total = n_k * n_g
    anywhere = pl.BlockSpec(memory_space=pltpu.HBM)
    dma = pltpu.SemaphoreType.DMA
    return pl.pallas_call(
        functools.partial(kernel, n_k, n_g),
        out_shape=jax.ShapeDtypeStruct((1, NSHIFT + 1, share * rows), F32),
        in_specs=[anywhere] * 5,
        out_specs=pl.BlockSpec(memory_space=pltpu.VMEM),
        scratch_shapes=[
            pltpu.VMEM(cond.shape, BF16),
            pltpu.VMEM(vale.shape, BF16),
            pltpu.SMEM(qtable.shape, jnp.int32),
            pltpu.VMEM(gmap.shape, jnp.int32),
            pltpu.VMEM((n_g, width, width), BF16),
            pltpu.VMEM((n_k, 2 * n_c, width), BF16),
            pltpu.VMEM((n_k * rows, width), BF16),
            pltpu.VMEM((n_k // 4, 4 * rows, 4 * rows), F32),
            pltpu.VMEM((total, share // 2, 2 * rows), F32),
            pltpu.VMEM((total, share // 2, 2 * rows), F32),
            dma((4,)), dma((n_g,)), dma((n_k,)), dma((n_k,)), dma((n_k,)), dma((n_k,)),
            dma((n_g,)), dma((n_g,)), dma(()), dma(()),
        ]
        + [pltpu.VMEM((n_k, 2 * n_c, width), BF16)] * n_g
        + [pltpu.VMEM((n_k * rows, width), BF16)] * n_g,
        compiler_params=pltpu.CompilerParams(
            collective_id=0, has_side_effects=True, vmem_limit_bytes=63 * 1024 * 1024
        ),
        cost_estimate=pl.CostEstimate(
            flops=2 * n_k * rows * width * screen.shape[2],
            bytes_accessed=2 * width * screen.shape[2],
            transcendentals=0,
        ),
    )(cond, vale, screen, qtable, gmap)


def solution(mesh):
    in_specs = (P("ka", None, "ga"), P("ka", None, "ga"), P("ka", "ga", None), P(), P("ka", "ga"))
    out_specs = P("ka", None, "ga")
    return jax.shard_map(
        per_device, mesh=mesh, in_specs=in_specs, out_specs=out_specs, check_vma=False
    )
```

```python
import functools

import jax
import jax.numpy as jnp
from jax import lax
from jax.experimental import pallas as pl
from jax.experimental.pallas import tpu as pltpu
from jax.sharding import PartitionSpec as P

NSHIFT = 2
MESH = pl.DeviceIdType.MESH
F32 = jnp.float32
BF16 = jnp.bfloat16


def flipped(index, bit):
    width = 1 << bit
    return index + width * (1 - 2 * ((index // width) % 2))


def moved(index, offset, bits):
    for bit in range(bits):
        if (offset >> bit) & 1:
            index = flipped(index, bit)
    return index


def densities(own, far):
    product = own.astype(F32)[:, None, :] * far.astype(F32)[None, :, :]
    return product.reshape(-1, own.shape[-1]).astype(BF16)


def kernel(
    n_k, n_g, cond_in, vale_in, screen, qtable_in, gmap_in, out,
    cond, vale, qtable, gmap, s_held, c_all, pc, tiles, sent, got,
    in_sem, s_sem, c_send, c_recv, v_send, v_recv, g_send, g_recv,
    t_send, t_recv, *blocks,
):
    v_from, w_from = blocks[:n_g], blocks[n_g:]
    bits = n_g.bit_length() - 1
    width = cond.shape[2]
    n_c = cond.shape[1]
    rows = n_c * n_c
    total = n_k * n_g
    me_k, me_g = lax.axis_index("ka"), lax.axis_index("ga")
    me = me_k * n_g + me_g

    arrivals = [
        pltpu.make_async_copy(source, target, in_sem.at[number])
        for number, (source, target) in enumerate(
            [(gmap_in, gmap), (cond_in, cond), (vale_in, vale), (qtable_in, qtable)]
        )
    ]
    for arrival in arrivals:
        arrival.start()

    depth = n_k // 2
    me_z, me_y = me_k // 2, me_k % 2
    other = me_z * 2 + 1 - me_y

    def along(step):
        return ((me_z + step) % depth) * 2 + me_y

    def beside(step):
        return ((me_z + step) % depth) * 2 + 1 - me_y

    barrier = pltpu.get_barrier_semaphore()
    peers = [(along(step), me_g) for step in range(1, depth)] + [(other, me_g)]
    peers += [(me_k, flipped(me_g, bit)) for bit in range(bits)]
    for peer in peers:
        pl.semaphore_signal(barrier, inc=1, device_id=peer, device_id_type=MESH)

    loads = []
    for offset in range(n_g):
        block = moved(me_g, offset, bits)
        load = pltpu.make_async_copy(
            screen.at[0, :, pl.ds(pl.multiple_of(block * width, width), width)],
            s_held.at[block],
            s_sem.at[offset],
        )
        load.start()
        loads.append(load)

    for arrival in arrivals:
        arrival.wait()

    local_map = gmap[...] - me_g * width
    both = jnp.concatenate([cond[0], vale[0]], axis=0)
    lanes = min(128, width)
    points = lax.broadcasted_iota(jnp.int32, (lanes, width), 0)
    pick = jnp.where(points == local_map % lanes, 1.0, 0.0).astype(BF16)
    stacked = jnp.concatenate(
        [both[:, first : first + lanes] for first in range(0, width, lanes)], axis=0
    )
    spread = jnp.dot(stacked, pick, preferred_element_type=F32)
    mapped = jnp.zeros((2 * n_c, width), F32)
    for number in range(width // lanes):
        piece = spread[number * 2 * n_c : (number + 1) * 2 * n_c]
        mapped = jnp.where(local_map // lanes == number, piece, mapped)
    mapped = mapped.astype(BF16)
    c_all[me_k] = jnp.concatenate([cond[0], mapped[:n_c]], axis=0)
    v_from[0][me_k] = jnp.concatenate([vale[0], mapped[n_c:]], axis=0)

    pl.semaphore_wait(barrier, len(peers))

    def c_copy(chunk, slot, target):
        return pltpu.make_async_remote_copy(
            src_ref=c_all.at[chunk], dst_ref=c_all.at[chunk],
            send_sem=c_send.at[slot], recv_sem=c_recv.at[chunk],
            device_id=(target, me_g), device_id_type=MESH,
        )

    def v_copy(chunk, slot, target):
        return pltpu.make_async_remote_copy(
            src_ref=v_from[0].at[chunk], dst_ref=v_from[0].at[chunk],
            send_sem=v_send.at[slot], recv_sem=v_recv.at[chunk],
            device_id=(target, me_g), device_id_type=MESH,
        )

    def across(chunk):
        for bit in reversed(range(bits)):
            pltpu.make_async_remote_copy(
                src_ref=v_from[0].at[chunk], dst_ref=v_from[1 << bit].at[chunk],
                send_sem=g_send.at[1 << bit], recv_sem=g_recv.at[1 << bit],
                device_id=(me_k, flipped(me_g, bit)), device_id_type=MESH,
            ).start()

    def whole_block(offset, bit):
        return pltpu.make_async_remote_copy(
            src_ref=v_from[offset], dst_ref=v_from[offset | (1 << bit)],
            send_sem=g_send.at[offset | (1 << bit)], recv_sem=g_recv.at[offset | (1 << bit)],
            device_id=(me_k, flipped(me_g, bit)), device_id_type=MESH,
        )

    for step in range(1, depth):
        c_copy(me_k, step - 1, along(step)).start()
    c_copy(me_k, depth - 1, other).start()
    across(me_k)
    for step in range(1, depth):
        v_copy(me_k, step - 1, along(step)).start()
    v_copy(me_k, depth - 1, other).start()
    for step in range(1, depth):
        c_copy(along(step), 0, other).wait_recv()
        c_copy(along(step), depth - 1 + step, other).start()
    for step in range(depth):
        c_copy(beside(step), 0, other).wait_recv()

    shift = jnp.int32(0)
    for row in range(n_k):
        shift = jnp.where(qtable[row, 0] == me_k, row, shift)

    def build(k, carry):
        partner = lax.rem(k - shift + n_k, n_k)
        dens = densities(c_all[k][:n_c], c_all[partner][n_c:])
        pc[pl.ds(pl.multiple_of(k * rows, rows), rows), :] = dens
        return carry

    lax.fori_loop(0, n_k, build, 0, unroll=4)
    tiles[...] = jnp.zeros_like(tiles)

    sub = min(512, width)
    unit = 8
    group = 4
    cuts = width // sub

    def work(weigh, close):
        if weigh is not None:
            block = moved(me_g, weigh, bits)
            loads[weigh].wait()

        def step(number, carry):
            which, column = number // cuts, number % cuts
            columns = pl.ds(pl.multiple_of(column * sub, sub), sub)
            all_rows = pl.ds(pl.multiple_of(which * (unit * rows), unit * rows), unit * rows)
            if weigh is not None:
                w_from[weigh][all_rows, columns] = jnp.dot(
                    pc[all_rows, :], s_held[block, :, columns], preferred_element_type=F32
                ).astype(BF16)
            if close is not None:
                for part in range(unit // group):
                    dens = []
                    for k in range(group):
                        k = which * unit + part * group + k
                        partner = lax.rem(k - shift + n_k, n_k)
                        own = v_from[close][k, :, columns][:n_c]
                        far = v_from[close][partner, :, columns][n_c:]
                        dens.append(densities(own, far))
                    first = pl.multiple_of((which * unit + part * group) * rows, group * rows)
                    tiles[which * (unit // group) + part] += lax.dot_general(
                        w_from[close][pl.ds(first, group * rows), columns],
                        jnp.concatenate(dens, axis=0),
                        (((1,), (1,)), ((), ())),
                        preferred_element_type=F32,
                    )
            return carry

        lax.fori_loop(0, (n_k // unit) * cuts, step, 0)

    passed = {0}

    def pass_on(offset):
        if offset in passed:
            return
        passed.add(offset)
        low = (offset & -offset).bit_length() - 1
        whole_block(offset & (offset - 1), low).wait_recv()
        for bit in reversed(range(low)):
            whole_block(offset, bit).start()

    order = sorted(range(n_g), key=lambda offset: (bin(offset).count("1"), offset))
    work(order[0], None)
    for step in range(1, depth):
        v_copy(along(step), 0, other).wait_recv()
        v_copy(along(step), depth - 1 + step, other).start()
        across(along(step))
    work(order[1], None)
    for step in range(depth):
        v_copy(beside(step), 0, other).wait_recv()
        across(beside(step))
    for number in range(2, n_g):
        if number > 2:
            pass_on(order[number - 2])
            pass_on(order[number - 1])
        work(order[number], order[number - 2])
    for offset in order[n_g - 2 :]:
        pass_on(offset)

    share = rows // n_g
    half = share // 2
    n_groups = n_k // group

    def finish(number, carry):
        which = (me_k // group + number) % n_groups
        tile = tiles[which]
        first = pl.multiple_of(which * (group * rows), group * rows)
        for close in order[n_g - 2 :]:
            for cut in range(cuts):
                columns = slice(cut * sub, (cut + 1) * sub)
                dens = []
                for k in range(group):
                    k = which * group + k
                    partner = lax.rem(k - shift + n_k, n_k)
                    own = v_from[close][k, :, columns][:n_c]
                    far = v_from[close][partner, :, columns][n_c:]
                    dens.append(densities(own, far))
                tile += lax.dot_general(
                    w_from[close][pl.ds(first, group * rows), columns],
                    jnp.concatenate(dens, axis=0),
                    (((1,), (1,)), ((), ())),
                    preferred_element_type=F32,
                )
        for k in range(group):
            for to in range(n_g):
                top = k * rows + to * share
                lanes = slice(k * rows, (k + 1) * rows)
                sent[(which * group + k) * n_g + to] = jnp.concatenate(
                    [tile[top : top + half, lanes], tile[top + half : top + share, lanes]],
                    axis=1,
                )

        def hand_out(step, carry):
            peer = which * (group * n_g) + step

            @pl.when(peer != me)
            def _():
                pltpu.make_async_remote_copy(
                    src_ref=sent.at[peer], dst_ref=got.at[me],
                    send_sem=t_send, recv_sem=t_recv,
                    device_id=(peer // n_g, peer % n_g), device_id_type=MESH,
                ).start()

            return carry

        lax.fori_loop(0, group * n_g, hand_out, 0)
        return carry

    lax.fori_loop(1, n_groups + 1, finish, 0)
    got[me] = sent[me]

    for slot in range(n_k - 1):
        c_copy(me_k, slot, other).wait_send()
        v_copy(me_k, slot, other).wait_send()
    for offset in range(1, n_g):
        low = (offset & -offset).bit_length() - 1
        whole_block(offset & (offset - 1), low).wait_send()

    handed = pltpu.make_async_remote_copy(
        src_ref=sent.at[pl.ds(0, total - 1)], dst_ref=got.at[pl.ds(0, total - 1)],
        send_sem=t_send, recv_sem=t_recv,
        device_id=(other, me_g), device_id_type=MESH,
    )
    handed.wait_recv()
    for number in range(NSHIFT + 1):
        holder = qtable[number, 0]
        value = got[holder * n_g]
        for source in range(1, n_g):
            value += got[holder * n_g + source]
        for row in range(share):
            side = row // half
            first = row - side * half
            out[0, number : number + 1, row * rows : (row + 1) * rows] = value[
                first : first + 1, side * rows : (side + 1) * rows
            ]
    handed.wait_send()


def per_device(cond, vale, screen, qtable, gmap):
    n_k, n_g = lax.axis_size("ka"), lax.axis_size("ga")
    n_c, width = cond.shape[1], cond.shape[2]
    rows = n_c * n_c
    share = rows // n_g
    total = n_k * n_g
    anywhere = pl.BlockSpec(memory_space=pltpu.HBM)
    dma = pltpu.SemaphoreType.DMA
    return pl.pallas_call(
        functools.partial(kernel, n_k, n_g),
        out_shape=jax.ShapeDtypeStruct((1, NSHIFT + 1, share * rows), F32),
        in_specs=[anywhere] * 5,
        out_specs=pl.BlockSpec(memory_space=pltpu.VMEM),
        scratch_shapes=[
            pltpu.VMEM(cond.shape, BF16),
            pltpu.VMEM(vale.shape, BF16),
            pltpu.SMEM(qtable.shape, jnp.int32),
            pltpu.VMEM(gmap.shape, jnp.int32),
            pltpu.VMEM((n_g, width, width), BF16),
            pltpu.VMEM((n_k, 2 * n_c, width), BF16),
            pltpu.VMEM((n_k * rows, width), BF16),
            pltpu.VMEM((n_k // 4, 4 * rows, 4 * rows), F32),
            pltpu.VMEM((total, share // 2, 2 * rows), F32),
            pltpu.VMEM((total, share // 2, 2 * rows), F32),
            dma((4,)), dma((n_g,)), dma((n_k,)), dma((n_k,)), dma((n_k,)), dma((n_k,)),
            dma((n_g,)), dma((n_g,)), dma(()), dma(()),
        ]
        + [pltpu.VMEM((n_k, 2 * n_c, width), BF16)] * n_g
        + [pltpu.VMEM((n_k * rows, width), BF16)] * n_g,
        compiler_params=pltpu.CompilerParams(
            collective_id=0, has_side_effects=True, vmem_limit_bytes=63 * 1024 * 1024
        ),
        cost_estimate=pl.CostEstimate(
            flops=2 * n_k * rows * width * screen.shape[2],
            bytes_accessed=2 * width * screen.shape[2],
            transcendentals=0,
        ),
    )(cond, vale, screen, qtable, gmap)


def solution(mesh):
    in_specs = (P("ka", None, "ga"), P("ka", None, "ga"), P("ka", "ga", None), P(), P("ka", "ga"))
    out_specs = P("ka", None, "ga")
    return jax.shard_map(
        per_device, mesh=mesh, in_specs=in_specs, out_specs=out_specs, check_vma=False
    )
```

```python
import functools

import jax
import jax.numpy as jnp
from jax import lax
from jax.experimental import pallas as pl
from jax.experimental.pallas import tpu as pltpu
from jax.sharding import PartitionSpec as P

NSHIFT = 2
MESH = pl.DeviceIdType.MESH
F32 = jnp.float32
BF16 = jnp.bfloat16


def flipped(index, bit):
    width = 1 << bit
    return index + width * (1 - 2 * ((index // width) % 2))


def moved(index, offset, bits):
    for bit in range(bits):
        if (offset >> bit) & 1:
            index = flipped(index, bit)
    return index


def densities(own, far):
    product = own.astype(F32)[:, None, :] * far.astype(F32)[None, :, :]
    return product.reshape(-1, own.shape[-1]).astype(BF16)


def kernel(
    n_k, n_g, cond_in, vale_in, screen, qtable_in, gmap_in, out,
    cond, vale, qtable, gmap, s_held, c_all, pc, tiles, sent, got,
    in_sem, s_sem, c_send, c_recv, v_send, v_recv, g_send, g_recv,
    t_send, t_recv, *blocks,
):
    v_from, w_from = blocks[:n_g], blocks[n_g:]
    bits = n_g.bit_length() - 1
    width = cond.shape[2]
    n_c = cond.shape[1]
    rows = n_c * n_c
    total = n_k * n_g
    me_k, me_g = lax.axis_index("ka"), lax.axis_index("ga")
    me = me_k * n_g + me_g

    arrivals = [
        pltpu.make_async_copy(source, target, in_sem.at[number])
        for number, (source, target) in enumerate(
            [(gmap_in, gmap), (cond_in, cond), (vale_in, vale), (qtable_in, qtable)]
        )
    ]
    for arrival in arrivals:
        arrival.start()

    depth = n_k // 2
    me_z, me_y = me_k // 2, me_k % 2
    other = me_z * 2 + 1 - me_y

    depth_bits = depth.bit_length() - 1
    far_first = sorted(range(1, depth), key=lambda step: step < 2)

    def along(step):
        return moved(me_z, step, depth_bits) * 2 + me_y

    def beside(step):
        return moved(me_z, step, depth_bits) * 2 + 1 - me_y

    barrier = pltpu.get_barrier_semaphore()
    peers = [(along(step), me_g) for step in range(1, depth)] + [(other, me_g)]
    peers += [(me_k, flipped(me_g, bit)) for bit in range(bits)]
    for peer in peers:
        pl.semaphore_signal(barrier, inc=1, device_id=peer, device_id_type=MESH)

    loads = []
    for offset in range(n_g):
        block = moved(me_g, offset, bits)
        load = pltpu.make_async_copy(
            screen.at[0, :, pl.ds(pl.multiple_of(block * width, width), width)],
            s_held.at[block],
            s_sem.at[offset],
        )
        load.start()
        loads.append(load)

    for arrival in arrivals:
        arrival.wait()

    local_map = gmap[...] - me_g * width
    both = jnp.concatenate([cond[0], vale[0]], axis=0)
    lanes = min(128, width)
    points = lax.broadcasted_iota(jnp.int32, (lanes, width), 0)
    pick = jnp.where(points == local_map % lanes, 1.0, 0.0).astype(BF16)
    stacked = jnp.concatenate(
        [both[:, first : first + lanes] for first in range(0, width, lanes)], axis=0
    )
    spread = jnp.dot(stacked, pick, preferred_element_type=F32)
    mapped = jnp.zeros((2 * n_c, width), F32)
    for number in range(width // lanes):
        piece = spread[number * 2 * n_c : (number + 1) * 2 * n_c]
        mapped = jnp.where(local_map // lanes == number, piece, mapped)
    mapped = mapped.astype(BF16)
    c_all[me_k] = jnp.concatenate([cond[0], mapped[:n_c]], axis=0)
    v_from[0][me_k] = jnp.concatenate([vale[0], mapped[n_c:]], axis=0)

    pl.semaphore_wait(barrier, len(peers))

    def c_copy(chunk, slot, target):
        return pltpu.make_async_remote_copy(
            src_ref=c_all.at[chunk], dst_ref=c_all.at[chunk],
            send_sem=c_send.at[slot], recv_sem=c_recv.at[chunk],
            device_id=(target, me_g), device_id_type=MESH,
        )

    def v_copy(chunk, slot, target):
        return pltpu.make_async_remote_copy(
            src_ref=v_from[0].at[chunk], dst_ref=v_from[0].at[chunk],
            send_sem=v_send.at[slot], recv_sem=v_recv.at[chunk],
            device_id=(target, me_g), device_id_type=MESH,
        )

    def across(chunk):
        for bit in reversed(range(bits)):
            pltpu.make_async_remote_copy(
                src_ref=v_from[0].at[chunk], dst_ref=v_from[1 << bit].at[chunk],
                send_sem=g_send.at[1 << bit], recv_sem=g_recv.at[1 << bit],
                device_id=(me_k, flipped(me_g, bit)), device_id_type=MESH,
            ).start()

    def whole_block(offset, bit):
        return pltpu.make_async_remote_copy(
            src_ref=v_from[offset], dst_ref=v_from[offset | (1 << bit)],
            send_sem=g_send.at[offset | (1 << bit)], recv_sem=g_recv.at[offset | (1 << bit)],
            device_id=(me_k, flipped(me_g, bit)), device_id_type=MESH,
        )

    for step in far_first:
        c_copy(me_k, step - 1, along(step)).start()
    c_copy(me_k, depth - 1, other).start()
    across(me_k)
    for step in range(1, depth):
        c_copy(along(step), 0, other).wait_recv()
        c_copy(along(step), depth - 1 + step, other).start()
    for step in far_first:
        v_copy(me_k, step - 1, along(step)).start()
    v_copy(me_k, depth - 1, other).start()
    for step in range(depth):
        c_copy(beside(step), 0, other).wait_recv()

    shift = jnp.int32(0)
    for row in range(n_k):
        shift = jnp.where(qtable[row, 0] == me_k, row, shift)

    def build(k, carry):
        partner = lax.rem(k - shift + n_k, n_k)
        dens = densities(c_all[k][:n_c], c_all[partner][n_c:])
        pc[pl.ds(pl.multiple_of(k * rows, rows), rows), :] = dens
        return carry

    lax.fori_loop(0, n_k, build, 0, unroll=4)
    tiles[...] = jnp.zeros_like(tiles)

    sub = min(512, width)
    unit = 8
    group = 4
    cuts = width // sub

    def work(weigh, close):
        if weigh is not None:
            block = moved(me_g, weigh, bits)
            loads[weigh].wait()

        def step(number, carry):
            which, column = number // cuts, number % cuts
            columns = pl.ds(pl.multiple_of(column * sub, sub), sub)
            all_rows = pl.ds(pl.multiple_of(which * (unit * rows), unit * rows), unit * rows)
            if weigh is not None:
                w_from[weigh][all_rows, columns] = jnp.dot(
                    pc[all_rows, :], s_held[block, :, columns], preferred_element_type=F32
                ).astype(BF16)
            if close is not None:
                for part in range(unit // group):
                    dens = []
                    for k in range(group):
                        k = which * unit + part * group + k
                        partner = lax.rem(k - shift + n_k, n_k)
                        own = v_from[close][k, :, columns][:n_c]
                        far = v_from[close][partner, :, columns][n_c:]
                        dens.append(densities(own, far))
                    first = pl.multiple_of((which * unit + part * group) * rows, group * rows)
                    tiles[which * (unit // group) + part] += lax.dot_general(
                        w_from[close][pl.ds(first, group * rows), columns],
                        jnp.concatenate(dens, axis=0),
                        (((1,), (1,)), ((), ())),
                        preferred_element_type=F32,
                    )
            return carry

        lax.fori_loop(0, (n_k // unit) * cuts, step, 0)

    passed = {0}

    def pass_on(offset):
        if offset in passed:
            return
        passed.add(offset)
        low = (offset & -offset).bit_length() - 1
        whole_block(offset & (offset - 1), low).wait_recv()
        for bit in reversed(range(low)):
            whole_block(offset, bit).start()

    order = sorted(range(n_g), key=lambda offset: (bin(offset).count("1"), offset))
    work(order[0], None)
    for step in range(1, depth):
        v_copy(along(step), 0, other).wait_recv()
        v_copy(along(step), depth - 1 + step, other).start()
        across(along(step))
    work(order[1], None)
    for step in range(depth):
        v_copy(beside(step), 0, other).wait_recv()
        across(beside(step))
    for number in range(2, n_g):
        if number > 2:
            pass_on(order[number - 2])
            pass_on(order[number - 1])
        work(order[number], order[number - 2])
    for offset in order[n_g - 2 :]:
        pass_on(offset)

    share = rows // n_g
    half = share // 2
    n_groups = n_k // group

    def finish(number, carry):
        which = (me_k // group + number) % n_groups
        tile = tiles[which]
        first = pl.multiple_of(which * (group * rows), group * rows)
        for close in order[n_g - 2 :]:
            for cut in range(cuts):
                columns = slice(cut * sub, (cut + 1) * sub)
                dens = []
                for k in range(group):
                    k = which * group + k
                    partner = lax.rem(k - shift + n_k, n_k)
                    own = v_from[close][k, :, columns][:n_c]
                    far = v_from[close][partner, :, columns][n_c:]
                    dens.append(densities(own, far))
                tile += lax.dot_general(
                    w_from[close][pl.ds(first, group * rows), columns],
                    jnp.concatenate(dens, axis=0),
                    (((1,), (1,)), ((), ())),
                    preferred_element_type=F32,
                )
        for k in range(group):
            for to in range(n_g):
                top = k * rows + to * share
                lanes = slice(k * rows, (k + 1) * rows)
                sent[(which * group + k) * n_g + to] = jnp.concatenate(
                    [tile[top : top + half, lanes], tile[top + half : top + share, lanes]],
                    axis=1,
                )

        def hand_out(step, carry):
            peer = which * (group * n_g) + step

            @pl.when(peer != me)
            def _():
                pltpu.make_async_remote_copy(
                    src_ref=sent.at[peer], dst_ref=got.at[me],
                    send_sem=t_send, recv_sem=t_recv,
                    device_id=(peer // n_g, peer % n_g), device_id_type=MESH,
                ).start()

            return carry

        lax.fori_loop(0, group * n_g, hand_out, 0)
        return carry

    lax.fori_loop(1, n_groups + 1, finish, 0)
    got[me] = sent[me]

    for slot in range(n_k - 1):
        c_copy(me_k, slot, other).wait_send()
        v_copy(me_k, slot, other).wait_send()
    for offset in range(1, n_g):
        low = (offset & -offset).bit_length() - 1
        whole_block(offset & (offset - 1), low).wait_send()

    handed = pltpu.make_async_remote_copy(
        src_ref=sent.at[pl.ds(0, total - 1)], dst_ref=got.at[pl.ds(0, total - 1)],
        send_sem=t_send, recv_sem=t_recv,
        device_id=(other, me_g), device_id_type=MESH,
    )
    handed.wait_recv()
    for number in range(NSHIFT + 1):
        holder = qtable[number, 0]
        value = got[holder * n_g]
        for source in range(1, n_g):
            value += got[holder * n_g + source]
        for row in range(share):
            side = row // half
            first = row - side * half
            out[0, number : number + 1, row * rows : (row + 1) * rows] = value[
                first : first + 1, side * rows : (side + 1) * rows
            ]
    handed.wait_send()


def per_device(cond, vale, screen, qtable, gmap):
    n_k, n_g = lax.axis_size("ka"), lax.axis_size("ga")
    n_c, width = cond.shape[1], cond.shape[2]
    rows = n_c * n_c
    share = rows // n_g
    total = n_k * n_g
    anywhere = pl.BlockSpec(memory_space=pltpu.HBM)
    dma = pltpu.SemaphoreType.DMA
    return pl.pallas_call(
        functools.partial(kernel, n_k, n_g),
        out_shape=jax.ShapeDtypeStruct((1, NSHIFT + 1, share * rows), F32),
        in_specs=[anywhere] * 5,
        out_specs=pl.BlockSpec(memory_space=pltpu.VMEM),
        scratch_shapes=[
            pltpu.VMEM(cond.shape, BF16),
            pltpu.VMEM(vale.shape, BF16),
            pltpu.SMEM(qtable.shape, jnp.int32),
            pltpu.VMEM(gmap.shape, jnp.int32),
            pltpu.VMEM((n_g, width, width), BF16),
            pltpu.VMEM((n_k, 2 * n_c, width), BF16),
            pltpu.VMEM((n_k * rows, width), BF16),
            pltpu.VMEM((n_k // 4, 4 * rows, 4 * rows), F32),
            pltpu.VMEM((total, share // 2, 2 * rows), F32),
            pltpu.VMEM((total, share // 2, 2 * rows), F32),
            dma((4,)), dma((n_g,)), dma((n_k,)), dma((n_k,)), dma((n_k,)), dma((n_k,)),
            dma((n_g,)), dma((n_g,)), dma(()), dma(()),
        ]
        + [pltpu.VMEM((n_k, 2 * n_c, width), BF16)] * n_g
        + [pltpu.VMEM((n_k * rows, width), BF16)] * n_g,
        compiler_params=pltpu.CompilerParams(
            collective_id=0, has_side_effects=True, vmem_limit_bytes=63 * 1024 * 1024
        ),
        cost_estimate=pl.CostEstimate(
            flops=2 * n_k * rows * width * screen.shape[2],
            bytes_accessed=2 * width * screen.shape[2],
            transcendentals=0,
        ),
    )(cond, vale, screen, qtable, gmap)


def solution(mesh):
    in_specs = (P("ka", None, "ga"), P("ka", None, "ga"), P("ka", "ga", None), P(), P("ka", "ga"))
    out_specs = P("ka", None, "ga")
    return jax.shard_map(
        per_device, mesh=mesh, in_specs=in_specs, out_specs=out_specs, check_vma=False
    )
```

```python
import functools

import jax
import jax.numpy as jnp
from jax import lax
from jax.experimental import pallas as pl
from jax.experimental.pallas import tpu as pltpu
from jax.sharding import PartitionSpec as P

NSHIFT = 2
MESH = pl.DeviceIdType.MESH
F32 = jnp.float32
BF16 = jnp.bfloat16


def flipped(index, bit):
    width = 1 << bit
    return index + width * (1 - 2 * ((index // width) % 2))


def moved(index, offset, bits):
    for bit in range(bits):
        if (offset >> bit) & 1:
            index = flipped(index, bit)
    return index


def densities(own, far):
    product = own.astype(F32)[:, None, :] * far.astype(F32)[None, :, :]
    return product.reshape(-1, own.shape[-1]).astype(BF16)


def kernel(
    n_k, n_g, cond_in, vale_in, screen, qtable_in, gmap_in, out,
    cond, vale, qtable, gmap, s_held, c_all, pc, tiles, sent, got,
    in_sem, s_sem, c_send, c_recv, v_send, v_recv, g_send, g_recv,
    t_send, t_recv, *blocks,
):
    v_from, w_from = blocks[:n_g], blocks[n_g:]
    bits = n_g.bit_length() - 1
    width = cond.shape[2]
    n_c = cond.shape[1]
    rows = n_c * n_c
    total = n_k * n_g
    me_k, me_g = lax.axis_index("ka"), lax.axis_index("ga")
    me = me_k * n_g + me_g

    arrivals = [
        pltpu.make_async_copy(source, target, in_sem.at[number])
        for number, (source, target) in enumerate(
            [(gmap_in, gmap), (cond_in, cond), (vale_in, vale), (qtable_in, qtable)]
        )
    ]
    for arrival in arrivals:
        arrival.start()

    depth = n_k // 2
    me_z, me_y = me_k // 2, me_k % 2
    other = me_z * 2 + 1 - me_y

    depth_bits = depth.bit_length() - 1
    far_first = sorted(range(1, depth), key=lambda step: step < 2)

    def along(step):
        return moved(me_z, step, depth_bits) * 2 + me_y

    def beside(step):
        return moved(me_z, step, depth_bits) * 2 + 1 - me_y

    barrier = pltpu.get_barrier_semaphore()
    peers = [(along(step), me_g) for step in range(1, depth)] + [(other, me_g)]
    peers += [(me_k, flipped(me_g, bit)) for bit in range(bits)]
    for peer in peers:
        pl.semaphore_signal(barrier, inc=1, device_id=peer, device_id_type=MESH)

    loads = []
    for offset in range(n_g):
        block = moved(me_g, offset, bits)
        load = pltpu.make_async_copy(
            screen.at[0, :, pl.ds(pl.multiple_of(block * width, width), width)],
            s_held.at[block],
            s_sem.at[offset],
        )
        load.start()
        loads.append(load)

    for arrival in arrivals:
        arrival.wait()

    local_map = gmap[...] - me_g * width
    both = jnp.concatenate([cond[0], vale[0]], axis=0)
    lanes = min(128, width)
    points = lax.broadcasted_iota(jnp.int32, (lanes, width), 0)
    pick = jnp.where(points == local_map % lanes, 1.0, 0.0).astype(BF16)
    stacked = jnp.concatenate(
        [both[:, first : first + lanes] for first in range(0, width, lanes)], axis=0
    )
    spread = jnp.dot(stacked, pick, preferred_element_type=F32)
    mapped = jnp.zeros((2 * n_c, width), F32)
    for number in range(width // lanes):
        piece = spread[number * 2 * n_c : (number + 1) * 2 * n_c]
        mapped = jnp.where(local_map // lanes == number, piece, mapped)
    mapped = mapped.astype(BF16)
    c_all[me_k] = jnp.concatenate([cond[0], mapped[:n_c]], axis=0)
    v_from[0][me_k] = jnp.concatenate([vale[0], mapped[n_c:]], axis=0)

    pl.semaphore_wait(barrier, len(peers))

    def c_copy(chunk, slot, target):
        return pltpu.make_async_remote_copy(
            src_ref=c_all.at[chunk], dst_ref=c_all.at[chunk],
            send_sem=c_send.at[slot], recv_sem=c_recv.at[chunk],
            device_id=(target, me_g), device_id_type=MESH,
        )

    def v_copy(chunk, slot, target):
        return pltpu.make_async_remote_copy(
            src_ref=v_from[0].at[chunk], dst_ref=v_from[0].at[chunk],
            send_sem=v_send.at[slot], recv_sem=v_recv.at[chunk],
            device_id=(target, me_g), device_id_type=MESH,
        )

    def across(chunk):
        for bit in reversed(range(bits)):
            pltpu.make_async_remote_copy(
                src_ref=v_from[0].at[chunk], dst_ref=v_from[1 << bit].at[chunk],
                send_sem=g_send.at[1 << bit], recv_sem=g_recv.at[1 << bit],
                device_id=(me_k, flipped(me_g, bit)), device_id_type=MESH,
            ).start()

    def whole_block(offset, bit):
        return pltpu.make_async_remote_copy(
            src_ref=v_from[offset], dst_ref=v_from[offset | (1 << bit)],
            send_sem=g_send.at[offset | (1 << bit)], recv_sem=g_recv.at[offset | (1 << bit)],
            device_id=(me_k, flipped(me_g, bit)), device_id_type=MESH,
        )

    for step in far_first:
        c_copy(me_k, step - 1, along(step)).start()
    c_copy(me_k, depth - 1, other).start()
    across(me_k)
    for step in range(1, depth):
        c_copy(along(step), 0, other).wait_recv()
        c_copy(along(step), depth - 1 + step, other).start()
    for step in far_first:
        v_copy(me_k, step - 1, along(step)).start()
    for step in range(depth):
        c_copy(beside(step), 0, other).wait_recv()
    v_copy(me_k, depth - 1, other).start()

    shift = jnp.int32(0)
    for row in range(n_k):
        shift = jnp.where(qtable[row, 0] == me_k, row, shift)

    def build(k, carry):
        partner = lax.rem(k - shift + n_k, n_k)
        dens = densities(c_all[k][:n_c], c_all[partner][n_c:])
        pc[pl.ds(pl.multiple_of(k * rows, rows), rows), :] = dens
        return carry

    lax.fori_loop(0, n_k, build, 0, unroll=4)
    tiles[...] = jnp.zeros_like(tiles)

    sub = min(512, width)
    unit = 8
    group = 4
    cuts = width // sub

    def work(weigh, close):
        if weigh is not None:
            block = moved(me_g, weigh, bits)
            loads[weigh].wait()

        def step(number, carry):
            which, column = number // cuts, number % cuts
            columns = pl.ds(pl.multiple_of(column * sub, sub), sub)
            all_rows = pl.ds(pl.multiple_of(which * (unit * rows), unit * rows), unit * rows)
            if weigh is not None:
                w_from[weigh][all_rows, columns] = jnp.dot(
                    pc[all_rows, :], s_held[block, :, columns], preferred_element_type=F32
                ).astype(BF16)
            if close is not None:
                for part in range(unit // group):
                    dens = []
                    for k in range(group):
                        k = which * unit + part * group + k
                        partner = lax.rem(k - shift + n_k, n_k)
                        own = v_from[close][k, :, columns][:n_c]
                        far = v_from[close][partner, :, columns][n_c:]
                        dens.append(densities(own, far))
                    first = pl.multiple_of((which * unit + part * group) * rows, group * rows)
                    tiles[which * (unit // group) + part] += lax.dot_general(
                        w_from[close][pl.ds(first, group * rows), columns],
                        jnp.concatenate(dens, axis=0),
                        (((1,), (1,)), ((), ())),
                        preferred_element_type=F32,
                    )
            return carry

        lax.fori_loop(0, (n_k // unit) * cuts, step, 0)

    passed = {0}

    def pass_on(offset):
        if offset in passed:
            return
        passed.add(offset)
        low = (offset & -offset).bit_length() - 1
        whole_block(offset & (offset - 1), low).wait_recv()
        for bit in reversed(range(low)):
            whole_block(offset, bit).start()

    order = sorted(range(n_g), key=lambda offset: (bin(offset).count("1"), offset))
    work(order[0], None)
    for step in range(1, depth):
        v_copy(along(step), 0, other).wait_recv()
        v_copy(along(step), depth - 1 + step, other).start()
        across(along(step))
    work(order[1], None)
    for step in range(depth):
        v_copy(beside(step), 0, other).wait_recv()
        across(beside(step))
    for number in range(2, n_g):
        if number > 2:
            pass_on(order[number - 2])
            pass_on(order[number - 1])
        work(order[number], order[number - 2])
    for offset in order[n_g - 2 :]:
        pass_on(offset)

    share = rows // n_g
    half = share // 2
    n_groups = n_k // group

    def finish(number, carry):
        which = (me_k // group + number) % n_groups
        tile = tiles[which]
        first = pl.multiple_of(which * (group * rows), group * rows)
        for close in order[n_g - 2 :]:
            for cut in range(cuts):
                columns = slice(cut * sub, (cut + 1) * sub)
                dens = []
                for k in range(group):
                    k = which * group + k
                    partner = lax.rem(k - shift + n_k, n_k)
                    own = v_from[close][k, :, columns][:n_c]
                    far = v_from[close][partner, :, columns][n_c:]
                    dens.append(densities(own, far))
                tile += lax.dot_general(
                    w_from[close][pl.ds(first, group * rows), columns],
                    jnp.concatenate(dens, axis=0),
                    (((1,), (1,)), ((), ())),
                    preferred_element_type=F32,
                )
        for k in range(group):
            for to in range(n_g):
                top = k * rows + to * share
                lanes = slice(k * rows, (k + 1) * rows)
                sent[(which * group + k) * n_g + to] = jnp.concatenate(
                    [tile[top : top + half, lanes], tile[top + half : top + share, lanes]],
                    axis=1,
                )

        def hand_out(step, carry):
            peer = which * (group * n_g) + step

            @pl.when(peer != me)
            def _():
                pltpu.make_async_remote_copy(
                    src_ref=sent.at[peer], dst_ref=got.at[me],
                    send_sem=t_send, recv_sem=t_recv,
                    device_id=(peer // n_g, peer % n_g), device_id_type=MESH,
                ).start()

            return carry

        lax.fori_loop(0, group * n_g, hand_out, 0, unroll=4)
        return carry

    lax.fori_loop(1, n_groups + 1, finish, 0)
    got[me] = sent[me]

    for slot in range(n_k - 1):
        c_copy(me_k, slot, other).wait_send()
        v_copy(me_k, slot, other).wait_send()
    for offset in range(1, n_g):
        low = (offset & -offset).bit_length() - 1
        whole_block(offset & (offset - 1), low).wait_send()

    handed = pltpu.make_async_remote_copy(
        src_ref=sent.at[pl.ds(0, total - 1)], dst_ref=got.at[pl.ds(0, total - 1)],
        send_sem=t_send, recv_sem=t_recv,
        device_id=(other, me_g), device_id_type=MESH,
    )
    handed.wait_recv()
    for number in range(NSHIFT + 1):
        holder = qtable[number, 0]
        value = got[holder * n_g]
        for source in range(1, n_g):
            value += got[holder * n_g + source]
        for row in range(share):
            side = row // half
            first = row - side * half
            out[0, number : number + 1, row * rows : (row + 1) * rows] = value[
                first : first + 1, side * rows : (side + 1) * rows
            ]
    handed.wait_send()


def per_device(cond, vale, screen, qtable, gmap):
    n_k, n_g = lax.axis_size("ka"), lax.axis_size("ga")
    n_c, width = cond.shape[1], cond.shape[2]
    rows = n_c * n_c
    share = rows // n_g
    total = n_k * n_g
    anywhere = pl.BlockSpec(memory_space=pltpu.HBM)
    dma = pltpu.SemaphoreType.DMA
    return pl.pallas_call(
        functools.partial(kernel, n_k, n_g),
        out_shape=jax.ShapeDtypeStruct((1, NSHIFT + 1, share * rows), F32),
        in_specs=[anywhere] * 5,
        out_specs=pl.BlockSpec(memory_space=pltpu.VMEM),
        scratch_shapes=[
            pltpu.VMEM(cond.shape, BF16),
            pltpu.VMEM(vale.shape, BF16),
            pltpu.SMEM(qtable.shape, jnp.int32),
            pltpu.VMEM(gmap.shape, jnp.int32),
            pltpu.VMEM((n_g, width, width), BF16),
            pltpu.VMEM((n_k, 2 * n_c, width), BF16),
            pltpu.VMEM((n_k * rows, width), BF16),
            pltpu.VMEM((n_k // 4, 4 * rows, 4 * rows), F32),
            pltpu.VMEM((total, share // 2, 2 * rows), F32),
            pltpu.VMEM((total, share // 2, 2 * rows), F32),
            dma((4,)), dma((n_g,)), dma((n_k,)), dma((n_k,)), dma((n_k,)), dma((n_k,)),
            dma((n_g,)), dma((n_g,)), dma(()), dma(()),
        ]
        + [pltpu.VMEM((n_k, 2 * n_c, width), BF16)] * n_g
        + [pltpu.VMEM((n_k * rows, width), BF16)] * n_g,
        compiler_params=pltpu.CompilerParams(
            collective_id=0, has_side_effects=True, vmem_limit_bytes=63 * 1024 * 1024
        ),
        cost_estimate=pl.CostEstimate(
            flops=2 * n_k * rows * width * screen.shape[2],
            bytes_accessed=2 * width * screen.shape[2],
            transcendentals=0,
        ),
    )(cond, vale, screen, qtable, gmap)


def solution(mesh):
    in_specs = (P("ka", None, "ga"), P("ka", None, "ga"), P("ka", "ga", None), P(), P("ka", "ga"))
    out_specs = P("ka", None, "ga")
    return jax.shard_map(
        per_device, mesh=mesh, in_specs=in_specs, out_specs=out_specs, check_vma=False
    )
```

```python
import functools

import jax
import jax.numpy as jnp
from jax import lax
from jax.experimental import pallas as pl
from jax.experimental.pallas import tpu as pltpu
from jax.sharding import PartitionSpec as P

NSHIFT = 2
MESH = pl.DeviceIdType.MESH
F32 = jnp.float32
BF16 = jnp.bfloat16


def flipped(index, bit):
    width = 1 << bit
    return index + width * (1 - 2 * ((index // width) % 2))


def moved(index, offset, bits):
    for bit in range(bits):
        if (offset >> bit) & 1:
            index = flipped(index, bit)
    return index


def densities(own, far):
    product = own.astype(F32)[:, None, :] * far.astype(F32)[None, :, :]
    return product.reshape(-1, own.shape[-1]).astype(BF16)


def kernel(
    n_k, n_g, cond_in, vale_in, screen, qtable_in, gmap_in, out,
    cond, vale, qtable, gmap, s_held, c_all, pc, tiles, sent, got,
    in_sem, s_sem, c_send, c_recv, v_send, v_recv, g_send, g_recv,
    t_send, t_recv, *blocks,
):
    v_from, w_from = blocks[:n_g], blocks[n_g:]
    bits = n_g.bit_length() - 1
    width = cond.shape[2]
    n_c = cond.shape[1]
    rows = n_c * n_c
    total = n_k * n_g
    me_k, me_g = lax.axis_index("ka"), lax.axis_index("ga")
    me = me_k * n_g + me_g

    arrivals = [
        pltpu.make_async_copy(source, target, in_sem.at[number])
        for number, (source, target) in enumerate(
            [(gmap_in, gmap), (cond_in, cond), (vale_in, vale), (qtable_in, qtable)]
        )
    ]
    for arrival in arrivals:
        arrival.start()

    depth = n_k // 2
    me_z, me_y = me_k // 2, me_k % 2
    other = me_z * 2 + 1 - me_y

    depth_bits = depth.bit_length() - 1
    far_first = sorted(range(1, depth), key=lambda step: step < 2)

    def along(step):
        return moved(me_z, step, depth_bits) * 2 + me_y

    def beside(step):
        return moved(me_z, step, depth_bits) * 2 + 1 - me_y

    barrier = pltpu.get_barrier_semaphore()
    peers = [(along(step), me_g) for step in range(1, depth)] + [(other, me_g)]
    peers += [(me_k, flipped(me_g, bit)) for bit in range(bits)]
    for peer in peers:
        pl.semaphore_signal(barrier, inc=1, device_id=peer, device_id_type=MESH)

    loads = []
    for offset in range(n_g):
        block = moved(me_g, offset, bits)
        load = pltpu.make_async_copy(
            screen.at[0, :, pl.ds(pl.multiple_of(block * width, width), width)],
            s_held.at[block],
            s_sem.at[offset],
        )
        load.start()
        loads.append(load)

    for arrival in arrivals:
        arrival.wait()

    local_map = gmap[...] - me_g * width
    both = jnp.concatenate([cond[0], vale[0]], axis=0)
    lanes = min(128, width)
    points = lax.broadcasted_iota(jnp.int32, (lanes, width), 0)
    pick = jnp.where(points == local_map % lanes, 1.0, 0.0).astype(BF16)
    stacked = jnp.concatenate(
        [both[:, first : first + lanes] for first in range(0, width, lanes)], axis=0
    )
    spread = jnp.dot(stacked, pick, preferred_element_type=F32)
    mapped = jnp.zeros((2 * n_c, width), F32)
    for number in range(width // lanes):
        piece = spread[number * 2 * n_c : (number + 1) * 2 * n_c]
        mapped = jnp.where(local_map // lanes == number, piece, mapped)
    mapped = mapped.astype(BF16)
    c_all[me_k] = jnp.concatenate([cond[0], mapped[:n_c]], axis=0)
    v_from[0][me_k] = jnp.concatenate([vale[0], mapped[n_c:]], axis=0)

    pl.semaphore_wait(barrier, len(peers))

    def c_copy(chunk, slot, target):
        return pltpu.make_async_remote_copy(
            src_ref=c_all.at[chunk], dst_ref=c_all.at[chunk],
            send_sem=c_send.at[slot], recv_sem=c_recv.at[chunk],
            device_id=(target, me_g), device_id_type=MESH,
        )

    def v_copy(chunk, slot, target):
        return pltpu.make_async_remote_copy(
            src_ref=v_from[0].at[chunk], dst_ref=v_from[0].at[chunk],
            send_sem=v_send.at[slot], recv_sem=v_recv.at[chunk],
            device_id=(target, me_g), device_id_type=MESH,
        )

    def across(chunk):
        for bit in reversed(range(bits)):
            pltpu.make_async_remote_copy(
                src_ref=v_from[0].at[chunk], dst_ref=v_from[1 << bit].at[chunk],
                send_sem=g_send.at[1 << bit], recv_sem=g_recv.at[1 << bit],
                device_id=(me_k, flipped(me_g, bit)), device_id_type=MESH,
            ).start()

    def whole_block(offset, bit):
        return pltpu.make_async_remote_copy(
            src_ref=v_from[offset], dst_ref=v_from[offset | (1 << bit)],
            send_sem=g_send.at[offset | (1 << bit)], recv_sem=g_recv.at[offset | (1 << bit)],
            device_id=(me_k, flipped(me_g, bit)), device_id_type=MESH,
        )

    for step in far_first:
        c_copy(me_k, step - 1, along(step)).start()
    c_copy(me_k, depth - 1, other).start()
    across(me_k)
    v_copy(me_k, depth - 1, other).start()
    for step in range(1, depth):
        c_copy(along(step), 0, other).wait_recv()
        c_copy(along(step), depth - 1 + step, other).start()
    for step in far_first:
        v_copy(me_k, step - 1, along(step)).start()
    for step in range(depth):
        c_copy(beside(step), 0, other).wait_recv()

    shift = jnp.int32(0)
    for row in range(n_k):
        shift = jnp.where(qtable[row, 0] == me_k, row, shift)

    def build(k, carry):
        partner = lax.rem(k - shift + n_k, n_k)
        dens = densities(c_all[k][:n_c], c_all[partner][n_c:])
        pc[pl.ds(pl.multiple_of(k * rows, rows), rows), :] = dens
        return carry

    lax.fori_loop(0, n_k, build, 0, unroll=4)
    tiles[...] = jnp.zeros_like(tiles)

    sub = min(512, width)
    unit = 8
    group = 4
    cuts = width // sub

    def work(weigh, close):
        if weigh is not None:
            block = moved(me_g, weigh, bits)
            loads[weigh].wait()

        def step(number, carry):
            which, column = number // cuts, number % cuts
            columns = pl.ds(pl.multiple_of(column * sub, sub), sub)
            all_rows = pl.ds(pl.multiple_of(which * (unit * rows), unit * rows), unit * rows)
            if weigh is not None:
                w_from[weigh][all_rows, columns] = jnp.dot(
                    pc[all_rows, :], s_held[block, :, columns], preferred_element_type=F32
                ).astype(BF16)
            if close is not None:
                for part in range(unit // group):
                    dens = []
                    for k in range(group):
                        k = which * unit + part * group + k
                        partner = lax.rem(k - shift + n_k, n_k)
                        own = v_from[close][k, :, columns][:n_c]
                        far = v_from[close][partner, :, columns][n_c:]
                        dens.append(densities(own, far))
                    first = pl.multiple_of((which * unit + part * group) * rows, group * rows)
                    tiles[which * (unit // group) + part] += lax.dot_general(
                        w_from[close][pl.ds(first, group * rows), columns],
                        jnp.concatenate(dens, axis=0),
                        (((1,), (1,)), ((), ())),
                        preferred_element_type=F32,
                    )
            return carry

        lax.fori_loop(0, (n_k // unit) * cuts, step, 0)

    passed = {0}

    def pass_on(offset):
        if offset in passed:
            return
        passed.add(offset)
        low = (offset & -offset).bit_length() - 1
        whole_block(offset & (offset - 1), low).wait_recv()
        for bit in reversed(range(low)):
            whole_block(offset, bit).start()

    order = sorted(range(n_g), key=lambda offset: (bin(offset).count("1"), offset))
    work(order[0], None)
    for step in range(1, depth):
        v_copy(along(step), 0, other).wait_recv()
        v_copy(along(step), depth - 1 + step, other).start()
        across(along(step))
    work(order[1], None)
    for step in range(depth):
        v_copy(beside(step), 0, other).wait_recv()
        across(beside(step))
    for number in range(2, n_g):
        if number > 2:
            pass_on(order[number - 2])
            pass_on(order[number - 1])
        work(order[number], order[number - 2])
    for offset in order[n_g - 2 :]:
        pass_on(offset)

    share = rows // n_g
    half = share // 2
    n_groups = n_k // group

    def finish(number, carry):
        which = (me_k // group + number) % n_groups
        tile = tiles[which]
        first = pl.multiple_of(which * (group * rows), group * rows)
        for close in order[n_g - 2 :]:
            for cut in range(cuts):
                columns = slice(cut * sub, (cut + 1) * sub)
                dens = []
                for k in range(group):
                    k = which * group + k
                    partner = lax.rem(k - shift + n_k, n_k)
                    own = v_from[close][k, :, columns][:n_c]
                    far = v_from[close][partner, :, columns][n_c:]
                    dens.append(densities(own, far))
                tile += lax.dot_general(
                    w_from[close][pl.ds(first, group * rows), columns],
                    jnp.concatenate(dens, axis=0),
                    (((1,), (1,)), ((), ())),
                    preferred_element_type=F32,
                )
        for k in range(group):
            for to in range(n_g):
                top = k * rows + to * share
                lanes = slice(k * rows, (k + 1) * rows)
                sent[(which * group + k) * n_g + to] = jnp.concatenate(
                    [tile[top : top + half, lanes], tile[top + half : top + share, lanes]],
                    axis=1,
                )

        def hand_out(step, carry):
            peer = which * (group * n_g) + step

            @pl.when(peer != me)
            def _():
                pltpu.make_async_remote_copy(
                    src_ref=sent.at[peer], dst_ref=got.at[me],
                    send_sem=t_send, recv_sem=t_recv,
                    device_id=(peer // n_g, peer % n_g), device_id_type=MESH,
                ).start()

            return carry

        lax.fori_loop(0, group * n_g, hand_out, 0)
        return carry

    lax.fori_loop(1, n_groups + 1, finish, 0)
    got[me] = sent[me]

    for slot in range(n_k - 1):
        c_copy(me_k, slot, other).wait_send()
        v_copy(me_k, slot, other).wait_send()
    for offset in range(1, n_g):
        low = (offset & -offset).bit_length() - 1
        whole_block(offset & (offset - 1), low).wait_send()

    handed = pltpu.make_async_remote_copy(
        src_ref=sent.at[pl.ds(0, total - 1)], dst_ref=got.at[pl.ds(0, total - 1)],
        send_sem=t_send, recv_sem=t_recv,
        device_id=(other, me_g), device_id_type=MESH,
    )
    handed.wait_recv()
    for number in range(NSHIFT + 1):
        holder = qtable[number, 0]
        value = got[holder * n_g]
        for source in range(1, n_g):
            value += got[holder * n_g + source]
        for row in range(share):
            side = row // half
            first = row - side * half
            out[0, number : number + 1, row * rows : (row + 1) * rows] = value[
                first : first + 1, side * rows : (side + 1) * rows
            ]
    handed.wait_send()


def per_device(cond, vale, screen, qtable, gmap):
    n_k, n_g = lax.axis_size("ka"), lax.axis_size("ga")
    n_c, width = cond.shape[1], cond.shape[2]
    rows = n_c * n_c
    share = rows // n_g
    total = n_k * n_g
    anywhere = pl.BlockSpec(memory_space=pltpu.HBM)
    dma = pltpu.SemaphoreType.DMA
    return pl.pallas_call(
        functools.partial(kernel, n_k, n_g),
        out_shape=jax.ShapeDtypeStruct((1, NSHIFT + 1, share * rows), F32),
        in_specs=[anywhere] * 5,
        out_specs=pl.BlockSpec(memory_space=pltpu.VMEM),
        scratch_shapes=[
            pltpu.VMEM(cond.shape, BF16),
            pltpu.VMEM(vale.shape, BF16),
            pltpu.SMEM(qtable.shape, jnp.int32),
            pltpu.VMEM(gmap.shape, jnp.int32),
            pltpu.VMEM((n_g, width, width), BF16),
            pltpu.VMEM((n_k, 2 * n_c, width), BF16),
            pltpu.VMEM((n_k * rows, width), BF16),
            pltpu.VMEM((n_k // 4, 4 * rows, 4 * rows), F32),
            pltpu.VMEM((total, share // 2, 2 * rows), F32),
            pltpu.VMEM((total, share // 2, 2 * rows), F32),
            dma((4,)), dma((n_g,)), dma((n_k,)), dma((n_k,)), dma((n_k,)), dma((n_k,)),
            dma((n_g,)), dma((n_g,)), dma(()), dma(()),
        ]
        + [pltpu.VMEM((n_k, 2 * n_c, width), BF16)] * n_g
        + [pltpu.VMEM((n_k * rows, width), BF16)] * n_g,
        compiler_params=pltpu.CompilerParams(
            collective_id=0, has_side_effects=True, vmem_limit_bytes=63 * 1024 * 1024
        ),
        cost_estimate=pl.CostEstimate(
            flops=2 * n_k * rows * width * screen.shape[2],
            bytes_accessed=2 * width * screen.shape[2],
            transcendentals=0,
        ),
    )(cond, vale, screen, qtable, gmap)


def solution(mesh):
    in_specs = (P("ka", None, "ga"), P("ka", None, "ga"), P("ka", "ga", None), P(), P("ka", "ga"))
    out_specs = P("ka", None, "ga")
    return jax.shard_map(
        per_device, mesh=mesh, in_specs=in_specs, out_specs=out_specs, check_vma=False
    )
```
